32 devices in a mesh: gen: 8 (over z, y), dat: 4 (over x, core).
Axes of the slice: x: 2, y: 2, z: 4, core: 2. Of those that a mesh axis runs over, the one named last changes fastest.
Arguments:
- gen_samples: bfloat16 [32768, 256], P(('gen', 'dat')), may hold values from -6 to 6
- data_samples: bfloat16 [3072, 256], P(('dat', 'gen')), may hold values from -6 to 6
- data_potential: float32 [3072], P(('dat', 'gen')), may hold values from -1 to 10
Outputs:
- gen_potential: float32 [32768], P(('gen', 'dat'))
- new_data_potential: float32 [3072], P(('dat', 'gen'))
The draws below stay inside these ranges and needn't reach their ends.
All inputs are finite; a program needn't handle non-finite values.
Results may differ from the reference program's by a relative error of at most 0.0003.
Values may be sent and summed in bfloat16 or wider, within the bound.
No kernel may reach another device: no remote copies, remote signals or barrier semaphores. Data moves between devices by JAX's collectives and lax.ppermute only.
A program may use at most 64 MiB of HBM per device.

```python
import jax
import jax.numpy as jnp
from jax import lax

D = 256
NG = 32768
NM = 3072


def draw_data_potential(key, part):
    key = jax.random.fold_in(key, 7)
    first = jax.random.fold_in(key, 0)
    values = jax.random.uniform(first, (NM,), jnp.float32, -1.0, 1.0)
    return values


def shard_levels(rng, dims, cuts, least, high):
    level = 1.0
    for dim, blocks in cuts:
        steps = jax.random.uniform(jax.random.fold_in(jax.random.fold_in(rng, 6), dim), (blocks,), jnp.float32, least / len(cuts), high / len(cuts))
        level = level * jnp.repeat(jnp.exp(steps), dims[dim] // blocks).reshape((-1,) + (1,) * (len(dims) - 1 - dim))
    return level


def bell_draw(own_key, shape, scale, bound, pieces=(), held_as=jnp.bfloat16):
    values = scale * jax.random.normal(own_key, shape, jnp.float32)
    if pieces:
        values = values * shard_levels(own_key, shape, pieces, -0.22, 0.18)
    return jnp.clip(values, -bound, bound).astype(held_as)


def setup_inputs(seed: int = 0) -> dict:
    keys = jax.random.split(jax.random.key(seed), 4)
    return {
        "gen_samples": bell_draw(keys[0], (NG, D), 1.0, 6.0, ((0, 32),)),
        "data_samples": bell_draw(keys[1], (NM, D), 1.0, 6.0, ((0, 32),)),
        "data_potential": draw_data_potential(jax.random.fold_in(keys[3], 71), 0),
    }


EPS = 0.05


def reference(gen_samples, data_samples, data_potential):
    width = gen_samples.shape[1]
    sq_data = jnp.sum(data_samples.astype(jnp.float32) ** 2, axis=1)
    block = min(512, NG)
    count = NG // block
    gen_blocks = gen_samples.reshape(count, block, width)

    def block_cost(rows):
        sq_rows = jnp.sum(rows.astype(jnp.float32) ** 2, axis=1)
        cross = jnp.dot(rows, data_samples.T, preferred_element_type=jnp.float32)
        return (sq_rows[:, None] + sq_data[None, :] - 2.0 * cross) / width

    def row_pass(rows):
        scores = (data_potential[None, :] - block_cost(rows)) / EPS
        top = jnp.max(scores, axis=1)
        total = jnp.sum(jnp.exp(scores - top[:, None]), axis=1)
        return -EPS * (top + jnp.log(total) - jnp.log(jnp.float32(NM)))

    gen_potential = lax.map(row_pass, gen_blocks).reshape(NG)

    def column_pass(carry, item):
        rows, pot = item
        run_max, run_sum = carry
        scores = (pot[:, None] - block_cost(rows)) / EPS
        top = jnp.maximum(run_max, jnp.max(scores, axis=0))
        run_sum = run_sum * jnp.exp(run_max - top) + jnp.sum(jnp.exp(scores - top[None, :]), axis=0)
        return (top, run_sum), None

    start = (jnp.full((NM,), -1e30, jnp.float32), jnp.zeros((NM,), jnp.float32))
    (col_max, col_sum), _ = lax.scan(column_pass, start, (gen_blocks, gen_potential.reshape(count, block)))
    new_data_potential = -EPS * (col_max + jnp.log(col_sum) - jnp.log(jnp.float32(NG)))
    return gen_potential, new_data_potential
```

```python
import functools
import math

import jax
import jax.numpy as jnp
from jax import lax
from jax.experimental import pallas as pl
from jax.experimental.pallas import tpu as pltpu
from jax.sharding import PartitionSpec as P

EPS = 0.05
LOG2E = 1.4426950408889634
LN2 = 0.6931471805599453
SCALE = LOG2E / EPS
ALL = ("dat", "gen")
LANES = 128


def lane_chunks(width, step):
    return [(start, min(step, width - start)) for start in range(0, width, step)]


def sinkhorn_kernel(x_ref, y_ref, b_ref, f_ref, col_ref, t_ref, max_ref, sum_ref, *, block, chunk, shares):
    rows, width = x_ref.shape
    cols = y_ref.shape[0]
    alpha = 2.0 * SCALE / width
    max_ref[...] = jnp.full(max_ref.shape, -jnp.inf, jnp.float32)
    sum_ref[...] = jnp.zeros(sum_ref.shape, jnp.float32)

    def fold(values, op):
        out = values[:, :LANES]
        for start in range(LANES, values.shape[1], LANES):
            out = op(out, values[:, start : start + LANES])
        return out

    def step(index, carry):
        x = x_ref[pl.ds(pl.multiple_of(index * block, block), block), :]
        top = None
        for start, size in lane_chunks(cols, chunk):
            dots = lax.dot_general(
                x, y_ref[start : start + size, :], (((1,), (1,)), ((), ())), preferred_element_type=jnp.float32
            )
            t = alpha * dots + b_ref[:, start : start + size]
            t_ref[:, start : start + size] = t
            part = fold(t, jnp.maximum)
            top = part if top is None else jnp.maximum(top, part)
        row_top = jnp.max(top, axis=1, keepdims=True)
        total = None
        for start, size in lane_chunks(cols, chunk):
            part = fold(jnp.exp2(t_ref[:, start : start + size] - row_top), jnp.add)
            total = part if total is None else total + part
        row_lse = row_top + jnp.log2(jnp.sum(total, axis=1, keepdims=True))
        x32 = x.astype(jnp.float32)
        sq = jnp.sum(x32 * x32, axis=1, keepdims=True)
        f = sq / width - (EPS * LN2) * row_lse + EPS * math.log(cols)
        wide = jnp.broadcast_to(f, (block, LANES))
        for part in range(block // LANES):
            turned = wide[part * LANES : (part + 1) * LANES, :].T
            f_ref[pl.ds(index * (block // LANES) + part, 1), :] = turned[0:1, :]
        for start, size in lane_chunks(cols, chunk):
            here = slice(start, start + size)
            u = t_ref[:, here] - row_lse
            old = max_ref[:, here]
            new = jnp.maximum(old, jnp.max(u, axis=0, keepdims=True))
            max_ref[:, here] = new
            sum_ref[:, here] = sum_ref[:, here] * jnp.exp2(old - new) + jnp.sum(
                jnp.exp2(u - new), axis=0, keepdims=True
            )
        return carry

    lax.fori_loop(0, rows // block, step, 0)
    max_ref[...] = max_ref[...] + jnp.log2(sum_ref[...]) - b_ref[...]
    share = cols // shares
    for k in range(shares):
        col_ref[k : k + 1, :] = max_ref[:, k * share : (k + 1) * share]


def per_device(gen_samples, data_samples, data_potential):
    rows, width = gen_samples.shape
    shares = lax.axis_size("dat") * lax.axis_size("gen")
    share = data_samples.shape[0]
    cols = share * shares
    wide = data_samples.astype(jnp.float32)
    sq_own = jnp.sum(wide * wide, axis=1)
    bias = SCALE * (data_potential - sq_own / width)
    everything = lax.all_gather(data_samples, ALL, axis=0, tiled=True)
    biases = lax.all_gather(bias, ALL, axis=0, tiled=True).reshape(1, cols)
    block = min(256, rows)
    kernel = functools.partial(sinkhorn_kernel, block=block, chunk=256, shares=shares)
    f, col = pl.pallas_call(
        kernel,
        out_shape=(
            jax.ShapeDtypeStruct((rows // LANES, LANES), jnp.float32),
            jax.ShapeDtypeStruct((shares, share), jnp.float32),
        ),
        scratch_shapes=[
            pltpu.VMEM((block, cols), jnp.float32),
            pltpu.VMEM((1, cols), jnp.float32),
            pltpu.VMEM((1, cols), jnp.float32),
        ],
        compiler_params=pltpu.CompilerParams(vmem_limit_bytes=48 * 1024 * 1024),
        cost_estimate=pl.CostEstimate(
            flops=2 * rows * cols * width, bytes_accessed=2 * (rows + cols) * width, transcendentals=2 * rows * cols
        ),
    )(gen_samples, everything, biases)
    parts = lax.all_to_all(col, ALL, 0, 0, tiled=True)
    top = jnp.max(parts, axis=0)
    total = top + jnp.log2(jnp.sum(jnp.exp2(parts - top[None, :]), axis=0))
    new_data = sq_own / width - (EPS * LN2) * total + EPS * math.log(rows * shares / cols)
    return f.reshape(rows), new_data


def solution(mesh):
    in_specs = (P(("gen", "dat"), None), P(("dat", "gen"), None), P(("dat", "gen")))
    out_specs = (P(("gen", "dat")), P(("dat", "gen")))
    return jax.shard_map(per_device, mesh=mesh, in_specs=in_specs, out_specs=out_specs, check_vma=False)
```

```python
import functools
import math

import jax
import jax.numpy as jnp
from jax import lax
from jax.experimental import pallas as pl
from jax.experimental.pallas import tpu as pltpu
from jax.sharding import PartitionSpec as P

EPS = 0.05
LOG2E = 1.4426950408889634
LN2 = 0.6931471805599453
SCALE = LOG2E / EPS
ALL = ("dat", "gen")
LANES = 128


def lane_chunks(width, step):
    return [(start, min(step, width - start)) for start in range(0, width, step)]


def exchanges(mesh_shape):
    steps = []
    for axis in ("gen", "dat"):
        bit = mesh_shape[axis] // 2
        while bit:
            steps.append((axis, bit))
            bit //= 2
    return steps


def swap(value, axis, bit):
    size = lax.axis_size(axis)
    return lax.ppermute(value, axis, [(k, k ^ bit) for k in range(size)])


def sinkhorn_kernel(x_ref, y_ref, b_rows_ref, f_ref, col_ref, t_ref, max_ref, sum_ref, b_ref, *, block, chunk, steps):
    rows, width = x_ref.shape
    cols = y_ref.shape[0]
    shares, share = b_rows_ref.shape
    for k in range(shares):
        b_ref[:, k * share : (k + 1) * share] = b_rows_ref[k : k + 1, :]
    alpha = 2.0 * SCALE / width
    max_ref[...] = jnp.full(max_ref.shape, -jnp.inf, jnp.float32)
    sum_ref[...] = jnp.zeros(sum_ref.shape, jnp.float32)

    def fold(values, op):
        out = values[:, :LANES]
        for start in range(LANES, values.shape[1], LANES):
            out = op(out, values[:, start : start + LANES])
        return out

    def step(index, carry):
        x = x_ref[pl.ds(pl.multiple_of(index * block, block), block), :]
        top = None
        for start, size in lane_chunks(cols, chunk):
            dots = lax.dot_general(
                x, y_ref[start : start + size, :], (((1,), (1,)), ((), ())), preferred_element_type=jnp.float32
            )
            t = alpha * dots + b_ref[:, start : start + size]
            t_ref[:, start : start + size] = t
            part = fold(t, jnp.maximum)
            top = part if top is None else jnp.maximum(top, part)
        row_top = jnp.max(top, axis=1, keepdims=True)
        total = None
        for start, size in lane_chunks(cols, chunk):
            part = fold(jnp.exp2(t_ref[:, start : start + size] - row_top), jnp.add)
            total = part if total is None else total + part
        row_lse = row_top + jnp.log2(jnp.sum(total, axis=1, keepdims=True))
        x32 = x.astype(jnp.float32)
        sq = jnp.sum(x32 * x32, axis=1, keepdims=True)
        f = sq / width - (EPS * LN2) * row_lse + EPS * math.log(cols)
        wide = jnp.broadcast_to(f, (block, LANES))
        for part in range(block // LANES):
            turned = wide[part * LANES : (part + 1) * LANES, :].T
            f_ref[pl.ds(index * (block // LANES) + part, 1), :] = turned[0:1, :]
        for start, size in lane_chunks(cols, chunk):
            here = slice(start, start + size)
            u = t_ref[:, here] - row_lse
            old = max_ref[:, here]
            new = jnp.maximum(old, jnp.max(u, axis=0, keepdims=True))
            max_ref[:, here] = new
            sum_ref[:, here] = sum_ref[:, here] * jnp.exp2(old - new) + jnp.sum(
                jnp.exp2(u - new), axis=0, keepdims=True
            )
        return carry

    lax.fori_loop(0, rows // block, step, 0)
    max_ref[...] = max_ref[...] + jnp.log2(sum_ref[...]) - b_ref[...]
    gen = lax.axis_index("gen")
    dat = lax.axis_index("dat")
    n_gen = lax.axis_size("gen")
    for k in range(shares):
        flips = {"gen": 0, "dat": 0}
        for place, (axis, bit) in enumerate(steps):
            if (k >> place) & 1:
                flips[axis] ^= bit
        owner = (dat ^ flips["dat"]) * n_gen + (gen ^ flips["gen"])
        col_ref[pl.ds(owner, 1), :] = max_ref[:, k * share : (k + 1) * share]


def per_device(gen_samples, data_samples, data_potential):
    rows, width = gen_samples.shape
    shares = lax.axis_size("dat") * lax.axis_size("gen")
    share = data_samples.shape[0]
    cols = share * shares
    wide = data_samples.astype(jnp.float32)
    sq_own = jnp.sum(wide * wide, axis=1)
    bias = SCALE * (data_potential - sq_own / width)
    everything = data_samples
    biases = bias.reshape(1, share)
    steps = exchanges({"gen": lax.axis_size("gen"), "dat": lax.axis_size("dat")})
    for axis, bit in steps:
        everything = jnp.concatenate([everything, swap(everything, axis, bit)], axis=0)
        biases = jnp.concatenate([biases, swap(biases, axis, bit)], axis=0)
    block = min(256, rows)
    kernel = functools.partial(sinkhorn_kernel, block=block, chunk=256, steps=steps)
    f, col = pl.pallas_call(
        kernel,
        out_shape=(
            jax.ShapeDtypeStruct((rows // LANES, LANES), jnp.float32),
            jax.ShapeDtypeStruct((shares, share), jnp.float32),
        ),
        scratch_shapes=[
            pltpu.VMEM((block, cols), jnp.float32),
            pltpu.VMEM((1, cols), jnp.float32),
            pltpu.VMEM((1, cols), jnp.float32),
            pltpu.VMEM((1, cols), jnp.float32),
        ],
        compiler_params=pltpu.CompilerParams(vmem_limit_bytes=48 * 1024 * 1024),
        cost_estimate=pl.CostEstimate(
            flops=2 * rows * cols * width, bytes_accessed=2 * (rows + cols) * width, transcendentals=2 * rows * cols
        ),
    )(gen_samples, everything, biases)
    parts = lax.all_to_all(col, ALL, 0, 0, tiled=True)
    top = jnp.max(parts, axis=0)
    total = top + jnp.log2(jnp.sum(jnp.exp2(parts - top[None, :]), axis=0))
    new_data = sq_own / width - (EPS * LN2) * total + EPS * math.log(rows * shares / cols)
    return f.reshape(rows), new_data


def solution(mesh):
    in_specs = (P(("gen", "dat"), None), P(("dat", "gen"), None), P(("dat", "gen")))
    out_specs = (P(("gen", "dat")), P(("dat", "gen")))
    return jax.shard_map(per_device, mesh=mesh, in_specs=in_specs, out_specs=out_specs, check_vma=False)
```

```python
import functools
import math

import jax
import jax.numpy as jnp
from jax import lax
from jax.experimental import pallas as pl
from jax.experimental.pallas import tpu as pltpu
from jax.sharding import PartitionSpec as P

EPS = 0.05
LOG2E = 1.4426950408889634
LN2 = 0.6931471805599453
SCALE = LOG2E / EPS
ALL = ("dat", "gen")
LANES = 128
TILE = 16


def lane_chunks(width, step):
    return [(start, min(step, width - start)) for start in range(0, width, step)]


def phases(n_gen, n_dat):
    far = [(mask, 0) for mask in range(2, n_gen, 2)]
    plane = [(g, d) for d in range(0, n_dat, 2) for g in range(2)][1:]
    return far, plane, [(0, 1)]


def swap(value, mask):
    n_gen, n_dat = lax.axis_size("gen"), lax.axis_size("dat")
    pairs = [
        (g * n_dat + d, (g ^ mask[0]) * n_dat + (d ^ mask[1])) for g in range(n_gen) for d in range(n_dat)
    ]
    return lax.ppermute(value, ("gen", "dat"), pairs)


def round_up(value, step):
    return -(-value // step) * step


def pack_kernel(y_ref, g_ref, packed_ref, sq_ref):
    share, width = y_ref.shape
    tall = packed_ref.shape[0] - TILE
    y = y_ref[...]
    wide = y.astype(jnp.float32)
    sq = jnp.sum(wide * wide, axis=1, keepdims=True)
    sq = jnp.broadcast_to(sq, (share, LANES)).T[0:1, :]
    sq_ref[...] = sq
    bias = SCALE * (g_ref[...] - sq / width)
    first = bias.astype(jnp.bfloat16).astype(jnp.float32)
    rest = bias - first
    second = rest.astype(jnp.bfloat16).astype(jnp.float32)
    third = rest - second
    row = lax.broadcasted_iota(jnp.int32, (TILE, share), 0)
    pieces = jnp.where(row == 0, first, jnp.where(row == 1, second, jnp.where(row == 2, third, 0.0)))
    if share < tall:
        packed_ref[...] = jnp.zeros(packed_ref.shape, jnp.bfloat16)
    else:
        packed_ref[tall:, :] = jnp.zeros((TILE, width), jnp.bfloat16)
    packed_ref[:share, :] = y
    packed_ref[tall:, :share] = pieces.astype(jnp.bfloat16)


def unpack(parts, share, y_ref, b_ref):
    tall = round_up(share, TILE)
    span = tall + TILE
    batch = TILE // math.gcd(share, TILE)
    held = []
    k = 0
    for part in parts:
        for start in range(0, part.shape[0], span):
            pieces = part[start + tall : start + span, :share].astype(jnp.float32)
            b_ref[:, k * share : (k + 1) * share] = pieces[0:1, :] + pieces[1:2, :] + pieces[2:3, :]
            if batch == 1:
                y_ref[k * share : (k + 1) * share, :] = part[start : start + share, :]
            else:
                held.append(part[start : start + tall, :].astype(jnp.float32)[:share, :])
                if len(held) == batch:
                    end = (k + 1) * share
                    y_ref[end - batch * share : end, :] = jnp.concatenate(held, axis=0).astype(jnp.bfloat16)
                    held = []
            k += 1


def sinkhorn_kernel(x_ref, *refs, block, chunk, masks):
    *parts, f_ref, col_ref, y_ref, t_ref, max_ref, sum_ref, b_ref = refs
    rows, width = x_ref.shape
    cols = y_ref.shape[0]
    share = col_ref.shape[1]
    unpack(parts, share, y_ref, b_ref)
    alpha = 2.0 * SCALE / width
    max_ref[...] = jnp.full(max_ref.shape, -jnp.inf, jnp.float32)
    sum_ref[...] = jnp.zeros(sum_ref.shape, jnp.float32)

    def fold(values, op):
        out = values[:, :LANES]
        for start in range(LANES, values.shape[1], LANES):
            out = op(out, values[:, start : start + LANES])
        return out

    def step(index, carry):
        x = x_ref[pl.ds(pl.multiple_of(index * block, block), block), :]
        top = None
        for start, size in lane_chunks(cols, chunk):
            dots = lax.dot_general(
                x, y_ref[start : start + size, :], (((1,), (1,)), ((), ())), preferred_element_type=jnp.float32
            )
            t = alpha * dots + b_ref[:, start : start + size]
            t_ref[:, start : start + size] = t
            part = fold(t, jnp.maximum)
            top = part if top is None else jnp.maximum(top, part)
        row_top = jnp.max(top, axis=1, keepdims=True)
        total = None
        for start, size in lane_chunks(cols, chunk):
            part = fold(jnp.exp2(t_ref[:, start : start + size] - row_top), jnp.add)
            total = part if total is None else total + part
        row_lse = row_top + jnp.log2(jnp.sum(total, axis=1, keepdims=True))
        x32 = x.astype(jnp.float32)
        sq = jnp.sum(x32 * x32, axis=1, keepdims=True)
        f = sq / width - (EPS * LN2) * row_lse + EPS * math.log(cols)
        wide = jnp.broadcast_to(f, (block, LANES))
        for part in range(block // LANES):
            turned = wide[part * LANES : (part + 1) * LANES, :].T
            f_ref[pl.ds(index * (block // LANES) + part, 1), :] = turned[0:1, :]
        for start, size in lane_chunks(cols, chunk):
            here = slice(start, start + size)
            u = t_ref[:, here] - row_lse
            old = max_ref[:, here]
            new = jnp.maximum(old, jnp.max(u, axis=0, keepdims=True))
            max_ref[:, here] = new
            sum_ref[:, here] = sum_ref[:, here] * jnp.exp2(old - new) + jnp.sum(
                jnp.exp2(u - new), axis=0, keepdims=True
            )
        return carry

    lax.fori_loop(0, rows // block, step, 0)
    max_ref[...] = max_ref[...] + jnp.log2(sum_ref[...]) - b_ref[...]
    gen = lax.axis_index("gen")
    dat = lax.axis_index("dat")
    n_gen = lax.axis_size("gen")
    for k, mask in enumerate(masks):
        owner = (dat ^ mask[1]) * n_gen + (gen ^ mask[0])
        col_ref[pl.ds(owner, 1), :] = max_ref[:, k * share : (k + 1) * share]


def per_device(gen_samples, data_samples, data_potential):
    rows, width = gen_samples.shape
    n_gen, n_dat = lax.axis_size("gen"), lax.axis_size("dat")
    shares = n_gen * n_dat
    share = data_samples.shape[0]
    cols = share * shares
    far, plane, pair = phases(n_gen, n_dat)
    packed, sq_own = pl.pallas_call(
        pack_kernel,
        out_shape=(
            jax.ShapeDtypeStruct((round_up(share, TILE) + TILE, width), jnp.bfloat16),
            jax.ShapeDtypeStruct((1, share), jnp.float32),
        ),
    )(data_samples, data_potential.reshape(1, share))
    column = jnp.concatenate([packed] + [swap(packed, m) for m in far], axis=0)
    half = [column] + [swap(column, m) for m in plane]
    parts = half + [swap(part, m) for m in pair for part in half]
    none = [(0, 0)]
    masks = [
        (a[0] ^ b[0] ^ c[0], a[1] ^ b[1] ^ c[1]) for c in none + pair for b in none + plane for a in none + far
    ]

    block = min(256, rows)
    kernel = functools.partial(sinkhorn_kernel, block=block, chunk=256, masks=masks)
    f, col = pl.pallas_call(
        kernel,
        out_shape=(
            jax.ShapeDtypeStruct((rows // LANES, LANES), jnp.float32),
            jax.ShapeDtypeStruct((shares, share), jnp.float32),
        ),
        scratch_shapes=[
            pltpu.VMEM((cols, width), jnp.bfloat16),
            pltpu.VMEM((block, cols), jnp.float32),
            pltpu.VMEM((1, cols), jnp.float32),
            pltpu.VMEM((1, cols), jnp.float32),
            pltpu.VMEM((1, cols), jnp.float32),
        ],
        compiler_params=pltpu.CompilerParams(vmem_limit_bytes=48 * 1024 * 1024),
        cost_estimate=pl.CostEstimate(
            flops=2 * rows * cols * width, bytes_accessed=2 * (rows + cols) * width, transcendentals=2 * rows * cols
        ),
    )(gen_samples, *parts)
    totals = lax.all_to_all(col, ALL, 0, 0, tiled=True)
    top = jnp.max(totals, axis=0)
    total = top + jnp.log2(jnp.sum(jnp.exp2(totals - top[None, :]), axis=0))
    new_data = sq_own[0] / width - (EPS * LN2) * total + EPS * math.log(rows * shares / cols)
    return f.reshape(rows), new_data


def solution(mesh):
    in_specs = (P(("gen", "dat"), None), P(("dat", "gen"), None), P(("dat", "gen")))
    out_specs = (P(("gen", "dat")), P(("dat", "gen")))
    return jax.shard_map(per_device, mesh=mesh, in_specs=in_specs, out_specs=out_specs, check_vma=False)
```

```python
import functools
import math

import jax
import jax.numpy as jnp
from jax import lax
from jax.experimental import pallas as pl
from jax.experimental.pallas import tpu as pltpu
from jax.sharding import PartitionSpec as P

EPS = 0.05
LOG2E = 1.4426950408889634
LN2 = 0.6931471805599453
SCALE = LOG2E / EPS
ALL = ("dat", "gen")
LANES = 128
TILE = 16


def lane_chunks(width, step):
    return [(start, min(step, width - start)) for start in range(0, width, step)]


def partners(n_gen, n_dat):
    far = [(g, 0) for g in range(2, n_gen, 2)]
    plane = [(g, d) for g in range(2) for d in range(0, n_dat, 2)][1:]
    return far, plane, (0, 1)


def swap(value, mask):
    n_gen, n_dat = lax.axis_size("gen"), lax.axis_size("dat")
    pairs = [
        (g * n_dat + d, (g ^ mask[0]) * n_dat + (d ^ mask[1])) for g in range(n_gen) for d in range(n_dat)
    ]
    return lax.ppermute(value, ("gen", "dat"), pairs)


def join(blocks):
    if len(blocks) == 1:
        return blocks[0]
    return jnp.concatenate([array for array, _ in blocks], axis=0), [m for _, masks in blocks for m in masks]


def sent(block, mask):
    array, masks = block
    return swap(array, mask), [(g ^ mask[0], d ^ mask[1]) for g, d in masks]


def gather(own, n_gen, n_dat):
    far, plane, pair = partners(n_gen, n_dat)
    own = (own, [(0, 0)])
    along = [sent(own, m) for m in far]
    across = [sent(own, m) for m in plane]
    straight = [m for m in plane if 0 in m]
    bent = [block for block, m in zip(across, plane) if 0 not in m]
    blocks = [own] + along + across
    twins = [sent(own, pair)]
    second = []
    column = join(along)
    second += [sent(column, m) for m in straight]
    if bent:
        corner = join(bent)
        second += [sent(corner, m) for m in far]
    twins += [sent(join(along + across), pair)]
    twins += [sent(block, pair) for block in second]
    return blocks + second + twins


def round_up(value, step):
    return -(-value // step) * step


def pack_kernel(y_ref, g_ref, packed_ref):
    share, width = y_ref.shape
    tall = packed_ref.shape[0] - TILE
    y = y_ref[...]
    wide = y.astype(jnp.float32)
    sq = jnp.sum(wide * wide, axis=1, keepdims=True)
    sq = jnp.broadcast_to(sq, (share, LANES)).T[0:1, :]
    bias = SCALE * (g_ref[...] - sq / width)
    first = bias.astype(jnp.bfloat16).astype(jnp.float32)
    rest = bias - first
    second = rest.astype(jnp.bfloat16).astype(jnp.float32)
    third = rest - second
    row = lax.broadcasted_iota(jnp.int32, (TILE, share), 0)
    pieces = jnp.where(row == 0, first, jnp.where(row == 1, second, jnp.where(row == 2, third, 0.0)))
    if share < tall:
        packed_ref[...] = jnp.zeros(packed_ref.shape, jnp.bfloat16)
    else:
        packed_ref[tall:, :] = jnp.zeros((TILE, width), jnp.bfloat16)
    packed_ref[:share, :] = y
    packed_ref[tall:, :share] = pieces.astype(jnp.bfloat16)


def unpack(parts, share, y_ref, b_ref):
    tall = round_up(share, TILE)
    span = tall + TILE
    batch = TILE // math.gcd(share, TILE)
    held = []
    k = 0
    for part in parts:
        for start in range(0, part.shape[0], span):
            pieces = part[start + tall : start + span, :share].astype(jnp.float32)
            b_ref[:, k * share : (k + 1) * share] = pieces[0:1, :] + pieces[1:2, :] + pieces[2:3, :]
            if batch == 1:
                y_ref[k * share : (k + 1) * share, :] = part[start : start + share, :]
            else:
                held.append(part[start : start + tall, :].astype(jnp.float32)[:share, :])
                if len(held) == batch:
                    end = (k + 1) * share
                    y_ref[end - batch * share : end, :] = jnp.concatenate(held, axis=0).astype(jnp.bfloat16)
                    held = []
            k += 1


def sinkhorn_kernel(x_ref, *refs, block, chunk, masks):
    *parts, f_ref, col_ref, y_ref, t_ref, max_ref, sum_ref, b_ref = refs
    rows, width = x_ref.shape
    cols = y_ref.shape[0]
    share = col_ref.shape[1]
    unpack(parts, share, y_ref, b_ref)
    alpha = 2.0 * SCALE / width
    max_ref[...] = jnp.full(max_ref.shape, -jnp.inf, jnp.float32)
    sum_ref[...] = jnp.zeros(sum_ref.shape, jnp.float32)

    def fold(values, op):
        out = values[:, :LANES]
        for start in range(LANES, values.shape[1], LANES):
            out = op(out, values[:, start : start + LANES])
        return out

    def step(index, carry):
        x = x_ref[pl.ds(pl.multiple_of(index * block, block), block), :]
        top = None
        for start, size in lane_chunks(cols, chunk):
            dots = lax.dot_general(
                x, y_ref[start : start + size, :], (((1,), (1,)), ((), ())), preferred_element_type=jnp.float32
            )
            t = alpha * dots + b_ref[:, start : start + size]
            t_ref[:, start : start + size] = t
            part = fold(t, jnp.maximum)
            top = part if top is None else jnp.maximum(top, part)
        row_top = jnp.max(top, axis=1, keepdims=True)
        total = None
        for start, size in lane_chunks(cols, chunk):
            part = fold(jnp.exp2(t_ref[:, start : start + size] - row_top), jnp.add)
            total = part if total is None else total + part
        row_lse = row_top + jnp.log2(jnp.sum(total, axis=1, keepdims=True))
        x32 = x.astype(jnp.float32)
        sq = jnp.sum(x32 * x32, axis=1, keepdims=True)
        f = sq / width - (EPS * LN2) * row_lse + EPS * math.log(cols)
        wide = jnp.broadcast_to(f, (block, LANES))
        for part in range(block // LANES):
            turned = wide[part * LANES : (part + 1) * LANES, :].T
            f_ref[pl.ds(index * (block // LANES) + part, 1), :] = turned[0:1, :]
        for start, size in lane_chunks(cols, chunk):
            here = slice(start, start + size)
            u = t_ref[:, here] - row_lse
            old = max_ref[:, here]
            new = jnp.maximum(old, jnp.max(u, axis=0, keepdims=True))
            max_ref[:, here] = new
            sum_ref[:, here] = sum_ref[:, here] * jnp.exp2(old - new) + jnp.sum(
                jnp.exp2(u - new), axis=0, keepdims=True
            )
        return carry

    lax.fori_loop(0, rows // block, step, 0)
    max_ref[...] = max_ref[...] + jnp.log2(sum_ref[...])
    gen = lax.axis_index("gen")
    dat = lax.axis_index("dat")
    n_gen = lax.axis_size("gen")
    for k, mask in enumerate(masks):
        owner = (dat ^ mask[1]) * n_gen + (gen ^ mask[0])
        col_ref[pl.ds(owner, 1), :] = max_ref[:, k * share : (k + 1) * share]


def per_device(gen_samples, data_samples, data_potential):
    rows, width = gen_samples.shape
    n_gen, n_dat = lax.axis_size("gen"), lax.axis_size("dat")
    shares = n_gen * n_dat
    share = data_samples.shape[0]
    cols = share * shares
    packed = pl.pallas_call(
        pack_kernel,
        out_shape=jax.ShapeDtypeStruct((round_up(share, TILE) + TILE, width), jnp.bfloat16),
    )(data_samples, data_potential.reshape(1, share))
    blocks = gather(packed, n_gen, n_dat)
    masks = [m for _, owners in blocks for m in owners]

    block = min(256, rows)
    kernel = functools.partial(sinkhorn_kernel, block=block, chunk=256, masks=masks)
    f, col = pl.pallas_call(
        kernel,
        out_shape=(
            jax.ShapeDtypeStruct((rows // LANES, LANES), jnp.float32),
            jax.ShapeDtypeStruct((shares, share), jnp.float32),
        ),
        scratch_shapes=[
            pltpu.VMEM((cols, width), jnp.bfloat16),
            pltpu.VMEM((block, cols), jnp.float32),
            pltpu.VMEM((1, cols), jnp.float32),
            pltpu.VMEM((1, cols), jnp.float32),
            pltpu.VMEM((1, cols), jnp.float32),
        ],
        compiler_params=pltpu.CompilerParams(vmem_limit_bytes=48 * 1024 * 1024),
        cost_estimate=pl.CostEstimate(
            flops=2 * rows * cols * width, bytes_accessed=2 * (rows + cols) * width, transcendentals=2 * rows * cols
        ),
    )(gen_samples, *[array for array, _ in blocks])
    totals = lax.all_to_all(col, ALL, 0, 0, tiled=True)
    top = jnp.max(totals, axis=0)
    total = top + jnp.log2(jnp.sum(jnp.exp2(totals - top[None, :]), axis=0))
    new_data = data_potential - (EPS * LN2) * total + EPS * math.log(rows * shares / cols)
    return f.reshape(rows), new_data


def solution(mesh):
    in_specs = (P(("gen", "dat"), None), P(("dat", "gen"), None), P(("dat", "gen")))
    out_specs = (P(("gen", "dat")), P(("dat", "gen")))
    return jax.shard_map(per_device, mesh=mesh, in_specs=in_specs, out_specs=out_specs, check_vma=False)
```

```python
import functools
import math

import jax
import jax.numpy as jnp
from jax import lax
from jax.experimental import pallas as pl
from jax.experimental.pallas import tpu as pltpu
from jax.sharding import PartitionSpec as P

EPS = 0.05
LOG2E = 1.4426950408889634
LN2 = 0.6931471805599453
SCALE = LOG2E / EPS
LANES = 128
TILE = 16
LIFT = 100.0
FLOOR = 2.0**-90
VMEM_LIMIT = 40 * 1024 * 1024


def round_up(value, step):
    return -(-value // step) * step


def swap(value, axis, mask):
    return lax.ppermute(value, axis, [(k, k ^ mask) for k in range(lax.axis_size(axis))])


def sent(block, axis, mask):
    array, masks = block
    return swap(array, axis, mask), [m ^ mask for m in masks]


def join(blocks):
    arrays = [array for array, _ in blocks]
    whole = arrays[0] if len(arrays) == 1 else jnp.concatenate(arrays, axis=0)
    return whole, [m for _, masks in blocks for m in masks]


def gather(gen_own, data_own):
    n_dat, n_gen = lax.axis_size("dat"), lax.axis_size("gen")
    gens = [(gen_own, [0])]
    bit = n_dat // 2
    while bit > 1:
        gens += [sent(block, "dat", bit) for block in gens]
        bit //= 2
    own = (data_own, [0])
    column = join([own] + [sent(own, "gen", m) for m in range(2, n_gen, 2)])
    parts = [column, sent(column, "gen", 1)]
    gens.insert(1, sent(gens[0], "dat", 1))
    held, _ = lax.optimization_barrier(([array for array, _ in gens[2:]], parts[1][0]))
    later = [sent((array, masks), "dat", 1) for array, (_, masks) in zip(held, gens[2:])]
    return gens, later, parts


def pack_kernel(y_ref, g_ref, packed_ref):
    share, width = y_ref.shape
    tall = packed_ref.shape[0] - TILE
    y = y_ref[...]
    wide = y.astype(jnp.float32)
    sq = jnp.sum(wide * wide, axis=1, keepdims=True)
    sq = jnp.broadcast_to(sq, (share, LANES)).T[0:1, :]
    bias = SCALE * (g_ref[...] - sq / width)
    first = bias.astype(jnp.bfloat16).astype(jnp.float32)
    rest = bias - first
    second = rest.astype(jnp.bfloat16).astype(jnp.float32)
    third = rest - second
    row = lax.broadcasted_iota(jnp.int32, (TILE, share), 0)
    pieces = jnp.where(row == 0, first, jnp.where(row == 1, second, jnp.where(row == 2, third, 0.0)))
    if share < tall:
        packed_ref[...] = jnp.zeros(packed_ref.shape, jnp.bfloat16)
    else:
        packed_ref[tall:, :] = jnp.zeros((TILE, width), jnp.bfloat16)
    packed_ref[:share, :] = y
    packed_ref[tall:, :share] = pieces.astype(jnp.bfloat16)


def unpack(parts, share, y_ref, b_ref):
    tall = round_up(share, TILE)
    span = tall + TILE
    batch = TILE // math.gcd(share, TILE)
    held = []
    k = 0
    for part in parts:
        for start in range(0, part.shape[0], span):
            pieces = part[start + tall : start + span, :share].astype(jnp.float32)
            bias = pieces[0:1, :] + pieces[1:2, :] + pieces[2:3, :]
            b_ref[k * share : (k + 1) * share, :] = jnp.broadcast_to(bias, (LANES, share)).T
            if batch == 1:
                y_ref[k * share : (k + 1) * share, :] = part[start : start + share, :]
            else:
                held.append(part[start : start + tall, :].astype(jnp.float32)[:share, :])
                if len(held) == batch:
                    end = (k + 1) * share
                    y_ref[end - batch * share : end, :] = jnp.concatenate(held, axis=0).astype(jnp.bfloat16)
                    held = []
            k += 1


def norm_kernel(x_ref, sq_ref):
    for k in range(sq_ref.shape[0]):
        x = x_ref[k * LANES : (k + 1) * LANES, :].astype(jnp.float32)
        sq = jnp.sum(x * x, axis=1, keepdims=True)
        sq_ref[k : k + 1, :] = jnp.broadcast_to(sq, (LANES, LANES)).T[0:1, :]


def spans(total, step):
    return [(start, min(step, total - start)) for start in range(0, total, step)]


def scores(y, x, bias, alpha):
    dots = lax.dot_general(y, x, (((1,), (1,)), ((), ())), preferred_element_type=jnp.float32)
    return alpha * dots + jnp.concatenate([bias] * (dots.shape[1] // LANES), axis=1)


def eight(values, op):
    groups = values.reshape(values.shape[0] // 8, 8, values.shape[1])
    return op(groups, axis=0)


def fold(values, op):
    out = values[:, :LANES]
    for start in range(LANES, values.shape[1], LANES):
        out = op(out, values[:, start : start + LANES])
    return out


def first_row_kernel(*refs, count, share, block, tall):
    xs, refs = refs[:count], refs[count:]
    *parts, l_ref, y_ref, b_ref, t_ref = refs
    unpack(parts, share, y_ref, b_ref)
    row_kernel(*xs, y_ref, b_ref, l_ref, t_ref, block=block, tall=tall)


def row_kernel(*refs, block, tall):
    *xs, y_ref, b_ref, l_ref, t_ref = refs
    cols, width = y_ref.shape
    rows = xs[0].shape[0]
    alpha = 2.0 * SCALE / width
    for place, x_ref in enumerate(xs):

        def step(index, carry, place=place, x_ref=x_ref):
            x = x_ref[pl.ds(pl.multiple_of(index * block, block), block), :]
            top = None
            for start, size in spans(cols, tall):
                here = slice(start, start + size)
                t = scores(y_ref[here, :], x, b_ref[here, :], alpha)
                t_ref[here, :] = t
                part = eight(t, jnp.max)
                top = part if top is None else jnp.maximum(top, part)
            top = jnp.max(top, axis=0, keepdims=True)
            total = None
            for start, size in spans(cols, tall):
                part = eight(jnp.exp2(t_ref[start : start + size, :] - top), jnp.sum)
                total = part if total is None else total + part
            log_sum = top + jnp.log2(jnp.sum(total, axis=0, keepdims=True))
            for k in range(block // LANES):
                row = (place * rows + index * block) // LANES + k
                l_ref[pl.ds(row, 1), :] = log_sum[:, k * LANES : (k + 1) * LANES]
            return carry

        lax.fori_loop(0, rows // block, step, 0)


def column_kernel(*refs, count, share, block, tall, orders, masks, log_cols):
    xs, refs = refs[:count], refs[count:]
    logs, refs = refs[: len(orders)], refs[len(orders) :]
    sq_ref, y_ref, b_ref, f_ref, col_ref, l_ref, sum_ref, top_ref = refs
    cols, width = y_ref.shape
    rows = xs[0].shape[0]
    alpha = 2.0 * SCALE / width
    tiles = rows // LANES
    for k in range(count):
        pieces = [log[order[k] * tiles : (order[k] + 1) * tiles, :] for log, order in zip(logs, orders)]
        top = functools.reduce(jnp.maximum, pieces)
        l_ref[k * tiles : (k + 1) * tiles, :] = top + jnp.log2(sum(jnp.exp2(piece - top) for piece in pieces))
    f_ref[...] = sq_ref[...] / width - (EPS * LN2) * l_ref[:tiles, :] + EPS * log_cols

    def each(visit):
        for place, x_ref in enumerate(xs):

            def step(index, carry, place=place, x_ref=x_ref):
                x = x_ref[pl.ds(pl.multiple_of(index * block, block), block), :]
                first = (place * rows + index * block) // LANES
                logs_here = [l_ref[pl.ds(first + k, 1), :] for k in range(block // LANES)]
                log_here = jnp.concatenate(logs_here, axis=1)
                for start, size in spans(cols, tall):
                    here = slice(start, start + size)
                    visit(here, scores(y_ref[here, :], x, b_ref[here, :], alpha) - log_here)
                return carry

            lax.fori_loop(0, rows // block, step, 0)

    def add(here, values):
        sum_ref[here, :] += fold(jnp.exp2(values + LIFT), jnp.add)

    def raise_top(here, values):
        top_ref[here, :] = jnp.maximum(top_ref[here, :], fold(values, jnp.maximum))

    def add_from_top(here, values):
        top = jnp.concatenate([top_ref[here, :]] * (block // LANES), axis=1)
        sum_ref[here, :] += fold(jnp.exp2(values - top), jnp.add)

    sum_ref[...] = jnp.zeros(sum_ref.shape, jnp.float32)
    each(add)
    least = jnp.min(jnp.sum(sum_ref[...], axis=1, keepdims=True))
    top_ref[...] = jnp.full(top_ref.shape, -LIFT, jnp.float32)

    @pl.when(jnp.logical_not(least >= FLOOR))
    def _():
        top_ref[...] = jnp.full(top_ref.shape, -jnp.inf, jnp.float32)
        each(raise_top)
        top = jnp.max(top_ref[...], axis=1, keepdims=True)
        top_ref[...] = jnp.broadcast_to(top, top_ref.shape)
        sum_ref[...] = jnp.zeros(sum_ref.shape, jnp.float32)
        each(add_from_top)

    gen = lax.axis_index("gen")
    for k, mask in enumerate(masks):
        here = slice(k * share, (k + 1) * share)
        total = jnp.sum(sum_ref[here, :].T, axis=0, keepdims=True)
        col_ref[pl.ds(gen ^ mask, 1), :] = top_ref[here, :].T[0:1, :] + jnp.log2(total)


def per_device(gen_samples, data_samples, data_potential):
    rows, width = gen_samples.shape
    n_gen, n_dat = lax.axis_size("gen"), lax.axis_size("dat")
    share = data_samples.shape[0]
    cols = share * n_gen
    tiles = rows // LANES
    params = pltpu.CompilerParams(vmem_limit_bytes=VMEM_LIMIT)
    packed = pl.pallas_call(
        pack_kernel,
        out_shape=jax.ShapeDtypeStruct((round_up(share, TILE) + TILE, width), jnp.bfloat16),
    )(data_samples, data_potential.reshape(1, share))
    early, late, parts = gather(gen_samples, packed)
    sq = pl.pallas_call(norm_kernel, out_shape=jax.ShapeDtypeStruct((tiles, LANES), jnp.float32))(gen_samples)
    order = [owners[0] for _, owners in early + late]
    masks = [m for _, owners in parts for m in owners]
    early, late, parts = [[array for array, _ in blocks] for blocks in (early, late, parts)]
    block = min(256, rows)
    tall = 128

    def cost(count):
        return pl.CostEstimate(
            flops=2 * rows * count * cols * width,
            bytes_accessed=2 * (rows * count + cols) * width,
            transcendentals=rows * count * cols,
        )

    scratch = [pltpu.VMEM((cols, block), jnp.float32)]
    log_early, y, bias = pl.pallas_call(
        functools.partial(first_row_kernel, count=len(early), share=share, block=block, tall=tall),
        out_shape=(
            jax.ShapeDtypeStruct((len(early) * tiles, LANES), jnp.float32),
            jax.ShapeDtypeStruct((cols, width), jnp.bfloat16),
            jax.ShapeDtypeStruct((cols, LANES), jnp.float32),
        ),
        scratch_shapes=scratch,
        compiler_params=params,
        cost_estimate=cost(len(early)),
    )(*early, *parts)
    log_late = pl.pallas_call(
        functools.partial(row_kernel, block=block, tall=tall),
        out_shape=jax.ShapeDtypeStruct((len(late) * tiles, LANES), jnp.float32),
        scratch_shapes=scratch,
        compiler_params=params,
        cost_estimate=cost(len(late)),
    )(*late, y, bias)
    log_own = jnp.concatenate([log_early, log_late], axis=0)
    logs = [log_own] + [swap(log_own, "dat", m) for m in order[1:]]
    orders = [[order.index(m ^ partner) for m in order] for partner in order]
    f, col = pl.pallas_call(
        functools.partial(
            column_kernel,
            count=n_dat,
            share=share,
            block=block,
            tall=tall,
            orders=orders,
            masks=masks,
            log_cols=math.log(cols * n_dat),
        ),
        out_shape=(
            jax.ShapeDtypeStruct((tiles, LANES), jnp.float32),
            jax.ShapeDtypeStruct((n_gen, share), jnp.float32),
        ),
        scratch_shapes=[
            pltpu.VMEM((n_dat * tiles, LANES), jnp.float32),
            pltpu.VMEM((cols, LANES), jnp.float32),
            pltpu.VMEM((cols, LANES), jnp.float32),
        ],
        compiler_params=params,
        cost_estimate=cost(n_dat),
    )(*early, *late, *logs, sq, y, bias)
    totals = lax.all_to_all(col, "gen", 0, 0, tiled=True)
    top = jnp.max(totals, axis=0)
    total = top + jnp.log2(jnp.sum(jnp.exp2(totals - top[None, :]), axis=0))
    new_data = data_potential - (EPS * LN2) * total + EPS * math.log(rows * n_gen / cols)
    return f.reshape(rows), new_data


def solution(mesh):
    in_specs = (P(("gen", "dat"), None), P(("dat", "gen"), None), P(("dat", "gen")))
    out_specs = (P(("gen", "dat")), P(("dat", "gen")))
    return jax.shard_map(per_device, mesh=mesh, in_specs=in_specs, out_specs=out_specs, check_vma=False)
```

```python
import functools
import math

import jax
import jax.numpy as jnp
from jax import lax
from jax.experimental import pallas as pl
from jax.experimental.pallas import tpu as pltpu
from jax.sharding import PartitionSpec as P

EPS = 0.05
LOG2E = 1.4426950408889634
LN2 = 0.6931471805599453
SCALE = LOG2E / EPS
LANES = 128
TILE = 16
LIFT = 100.0
FLOOR = 2.0**-90
VMEM_LIMIT = 40 * 1024 * 1024


def round_up(value, step):
    return -(-value // step) * step


def swap(value, axis, mask):
    return lax.ppermute(value, axis, [(k, k ^ mask) for k in range(lax.axis_size(axis))])


def gather(gen_own, message, column):
    n_dat, n_gen = lax.axis_size("dat"), lax.axis_size("gen")
    gens = [(gen_own, [0])]
    bit = n_dat // 2
    while bit > 1:
        gens += [(swap(array, "dat", bit), [m ^ bit for m in masks]) for array, masks in gens]
        bit //= 2
    span = message.shape[0]
    far = range(2, n_gen, 2)
    for k, mask in enumerate(far):
        column = lax.dynamic_update_slice(column, swap(message, "gen", mask), ((k + 1) * span, 0))
    masks = [(m, 0) for m in [0, *far]]
    near = swap(column, "gen", 1), [(g ^ 1, d) for g, d in masks]
    parts = [(column, masks), near]
    return gens, parts + [(swap(array, "dat", 1), [(g, 1) for g, _ in masks]) for array, masks in parts]


def pack_kernel(y_ref, g_ref, packed_ref, column_ref):
    share, width = y_ref.shape
    tall = packed_ref.shape[0] - TILE
    y = y_ref[...]
    wide = y.astype(jnp.float32)
    sq = jnp.sum(wide * wide, axis=1, keepdims=True)
    sq = jnp.broadcast_to(sq, (share, LANES)).T[0:1, :]
    bias = SCALE * (g_ref[...] - sq / width)
    first = bias.astype(jnp.bfloat16).astype(jnp.float32)
    rest = bias - first
    second = rest.astype(jnp.bfloat16).astype(jnp.float32)
    third = rest - second
    row = lax.broadcasted_iota(jnp.int32, (TILE, share), 0)
    pieces = jnp.where(row == 0, first, jnp.where(row == 1, second, jnp.where(row == 2, third, 0.0)))
    if share < tall:
        packed_ref[...] = jnp.zeros(packed_ref.shape, jnp.bfloat16)
    else:
        packed_ref[tall:, :] = jnp.zeros((TILE, width), jnp.bfloat16)
    packed_ref[:share, :] = y
    packed_ref[tall:, :share] = pieces.astype(jnp.bfloat16)
    column_ref[: packed_ref.shape[0], :] = packed_ref[...]


def unpack(parts, share, y_ref, b_ref):
    tall = round_up(share, TILE)
    span = tall + TILE
    batch = TILE // math.gcd(share, TILE)
    held = []
    k = 0
    for part in parts:
        for start in range(0, part.shape[0], span):
            pieces = part[start + tall : start + span, :share].astype(jnp.float32)
            bias = pieces[0:1, :] + pieces[1:2, :] + pieces[2:3, :]
            b_ref[k * share : (k + 1) * share, :] = jnp.broadcast_to(bias, (LANES, share)).T
            if batch == 1:
                y_ref[k * share : (k + 1) * share, :] = part[start : start + share, :]
            else:
                held.append(part[start : start + tall, :].astype(jnp.float32)[:share, :])
                if len(held) == batch:
                    end = (k + 1) * share
                    y_ref[end - batch * share : end, :] = jnp.concatenate(held, axis=0).astype(jnp.bfloat16)
                    held = []
            k += 1


def norm_kernel(x_ref, sq_ref):
    x = x_ref[...].astype(jnp.float32)
    square = x * x
    high = square.astype(jnp.bfloat16)
    low = (square - high.astype(jnp.float32)).astype(jnp.bfloat16)
    ones = jnp.ones((TILE, x.shape[1]), jnp.bfloat16)
    sq = jnp.zeros((TILE, x.shape[0]), jnp.float32)
    for half in (high, low):
        sq += lax.dot_general(ones, half, (((1,), (1,)), ((), ())), preferred_element_type=jnp.float32)
    for k in range(sq_ref.shape[0]):
        sq_ref[k : k + 1, :] = sq[0:1, k * LANES : (k + 1) * LANES]


def spans(total, step):
    return [(start, min(step, total - start)) for start in range(0, total, step)]


def dots(y, x):
    return lax.dot_general(y, x, (((1,), (1,)), ((), ())), preferred_element_type=jnp.float32)


def across(values, count):
    return jnp.concatenate([values] * count, axis=1)


def each_pair(xs, block, dots_ref, fill, visit):
    rows = xs[0].shape[0]
    pair = 2 if rows // block % 2 == 0 else 1
    for place, x_ref in enumerate(xs):

        def step(index, carry, place=place, x_ref=x_ref):
            firsts = [(index * pair + k) * block for k in range(pair)]
            for k, first in enumerate(firsts):
                fill(dots_ref.at[k], x_ref[pl.ds(pl.multiple_of(first, block), block), :])
            for k, first in enumerate(firsts):
                visit(dots_ref.at[k], (place * rows + first) // LANES)
            return carry

        lax.fori_loop(0, rows // block // pair, step, 0)


def eight(values, op):
    groups = values.reshape(values.shape[0] // 8, 8, values.shape[1])
    return op(groups, axis=0)


def fold(values, op):
    out = values[:, :LANES]
    for start in range(LANES, values.shape[1], LANES):
        out = op(out, values[:, start : start + LANES])
    return out


def row_kernel(*refs, count, share, block, tall, merge):
    xs, refs = refs[:count], refs[count:]
    *parts, l_ref, y_ref, b_ref, t_ref = refs
    before = parts.pop() if merge else None
    unpack(parts, share, y_ref, b_ref)
    cols, width = y_ref.shape
    alpha = 2.0 * SCALE / width
    repeat = block // LANES

    def fill(slot, x):
        slot[...] = dots(y_ref[...], x)

    def visit(slot, place):
        top = None
        for start, size in spans(cols, tall):
            here = slice(start, start + size)
            t = alpha * slot[here, :] + across(b_ref[here, :], repeat)
            slot[here, :] = t
            part = eight(t, jnp.max)
            top = part if top is None else jnp.maximum(top, part)
        top = jnp.max(top, axis=0, keepdims=True)
        total = None
        for start, size in spans(cols, tall):
            part = eight(jnp.exp2(slot[start : start + size, :] - top), jnp.sum)
            total = part if total is None else total + part
        log_sum = top + jnp.log2(jnp.sum(total, axis=0, keepdims=True))
        for k in range(repeat):
            l_ref[pl.ds(place + k, 1), :] = log_sum[:, k * LANES : (k + 1) * LANES]

    each_pair(xs, block, t_ref, fill, visit)
    if merge:
        l_ref[...] = merged([before[...], l_ref[...]])


def merged(pieces):
    top = functools.reduce(jnp.maximum, pieces)
    return top + jnp.log2(sum(jnp.exp2(piece - top) for piece in pieces))


def column_kernel(*refs, count, share, block, tall, orders, masks, log_cols):
    xs, refs = refs[:count], refs[count:]
    logs, refs = refs[: len(orders)], refs[len(orders) :]
    sq_ref, g_ref, *data, f_ref, own_g_ref, col_ref, l_ref, sum_ref, top_ref, t_ref = refs
    ys, biases = data[::2], data[1::2]
    rows, width = xs[0].shape
    alpha = 2.0 * SCALE / width
    repeat = block // LANES
    tiles = rows // LANES
    for k in range(count):
        pieces = [log[order[k] * tiles : (order[k] + 1) * tiles, :] for log, order in zip(logs, orders)]
        l_ref[k * tiles : (k + 1) * tiles, :] = merged(pieces)
    own_g_ref[...] = g_ref[...]
    f_ref[...] = sq_ref[...] / width - (EPS * LN2) * l_ref[:tiles, :] + EPS * log_cols

    def fill(slot, x):
        offset = 0
        for y_ref in ys:
            cols = y_ref.shape[0]
            slot[offset : offset + cols, :] = dots(y_ref[...], x)
            offset += cols

    def each(lift, visit):
        def visit_all(slot, place):
            log_here = jnp.concatenate([l_ref[pl.ds(place + k, 1), :] for k in range(repeat)], axis=1) - lift
            offset = 0
            for b_ref in biases:
                for start, size in spans(b_ref.shape[0], tall):
                    here = slice(offset + start, offset + start + size)
                    bias = across(b_ref[start : start + size, :], repeat)
                    visit(here, alpha * slot[here, :] + bias - log_here)
                offset += b_ref.shape[0]

        each_pair(xs, block, t_ref, fill, visit_all)

    def add(here, values):
        sum_ref[here, :] += fold(jnp.exp2(values), jnp.add)

    def raise_top(here, values):
        top_ref[here, :] = jnp.maximum(top_ref[here, :], fold(values, jnp.maximum))

    def add_from_top(here, values):
        sum_ref[here, :] += fold(jnp.exp2(values - across(top_ref[here, :], repeat)), jnp.add)

    sum_ref[...] = jnp.zeros(sum_ref.shape, jnp.float32)
    each(LIFT, add)
    least = jnp.min(jnp.sum(sum_ref[...], axis=1, keepdims=True))
    top_ref[...] = jnp.full(top_ref.shape, -LIFT, jnp.float32)

    @pl.when(jnp.logical_not(least >= FLOOR))
    def _():
        top_ref[...] = jnp.full(top_ref.shape, -jnp.inf, jnp.float32)
        each(0.0, raise_top)
        top = jnp.max(top_ref[...], axis=1, keepdims=True)
        top_ref[...] = jnp.broadcast_to(top, top_ref.shape)
        sum_ref[...] = jnp.zeros(sum_ref.shape, jnp.float32)
        each(0.0, add_from_top)

    gen, core = lax.axis_index("gen"), lax.rem(lax.axis_index("dat"), 2)
    n_gen = lax.axis_size("gen")
    for k, mask in enumerate(masks):
        here = slice(k * share, (k + 1) * share)
        total = jnp.sum(sum_ref[here, :].T, axis=0, keepdims=True)
        place = ((core ^ mask[1]) * n_gen) + (gen ^ mask[0])
        col_ref[pl.ds(place, 1), :] = top_ref[here, :].T[0:1, :] + jnp.log2(total)


def per_device(gen_samples, data_samples, data_potential):
    rows, width = gen_samples.shape
    n_gen, n_dat = lax.axis_size("gen"), lax.axis_size("dat")
    share = data_samples.shape[0]
    half = share * n_gen
    cols = 2 * half
    tiles = rows // LANES
    span = round_up(share, TILE) + TILE
    own_g = data_potential.reshape(1, share)
    params = pltpu.CompilerParams(vmem_limit_bytes=VMEM_LIMIT)
    message, column = pl.pallas_call(
        pack_kernel,
        out_shape=(
            jax.ShapeDtypeStruct((span, width), jnp.bfloat16),
            jax.ShapeDtypeStruct((span * (n_gen // 2), width), jnp.bfloat16),
        ),
    )(data_samples, own_g)
    gens, parts = gather(gen_samples, message, column)
    sq = pl.pallas_call(norm_kernel, out_shape=jax.ShapeDtypeStruct((tiles, LANES), jnp.float32))(gen_samples)
    order = [owners[0] for _, owners in gens]
    masks = [m for _, owners in parts for m in owners]
    xs = [array for array, _ in gens]
    parts = [array for array, _ in parts]
    block = min(256, rows)
    tall = 64
    pair = 2 if rows // block % 2 == 0 else 1

    def cost(count):
        return pl.CostEstimate(
            flops=2 * rows * len(xs) * count * width,
            bytes_accessed=2 * (rows * len(xs) + count) * width,
            transcendentals=rows * len(xs) * count,
        )

    logs = []
    data = []
    for some in (parts[:3], parts[3:]):
        count = len(some) * half // 2
        log, y, bias = pl.pallas_call(
            functools.partial(
                row_kernel, count=len(xs), share=share, block=block, tall=tall, merge=bool(logs)
            ),
            out_shape=(
                jax.ShapeDtypeStruct((len(xs) * tiles, LANES), jnp.float32),
                jax.ShapeDtypeStruct((count, width), jnp.bfloat16),
                jax.ShapeDtypeStruct((count, LANES), jnp.float32),
            ),
            scratch_shapes=[pltpu.VMEM((pair, count, block), jnp.float32)],
            compiler_params=params,
            cost_estimate=cost(count),
        )(*xs, *some, *logs)
        logs = [log]
        data += [y, bias]
    logs += [swap(logs[0], "dat", m) for m in order[1:]]
    orders = [[order.index(m ^ partner) for m in order] for partner in order]
    f, own_g, col = pl.pallas_call(
        functools.partial(
            column_kernel,
            count=len(xs),
            share=share,
            block=block,
            tall=tall,
            orders=orders,
            masks=masks,
            log_cols=math.log(half * n_dat),
        ),
        out_shape=(
            jax.ShapeDtypeStruct((tiles, LANES), jnp.float32),
            jax.ShapeDtypeStruct((1, share), jnp.float32),
            jax.ShapeDtypeStruct((2 * n_gen, share), jnp.float32),
        ),
        scratch_shapes=[
            pltpu.VMEM((len(xs) * tiles, LANES), jnp.float32),
            pltpu.VMEM((cols, LANES), jnp.float32),
            pltpu.VMEM((cols, LANES), jnp.float32),
            pltpu.VMEM((pair, cols, block), jnp.float32),
        ],
        compiler_params=params,
        cost_estimate=cost(cols),
    )(*xs, *logs, sq, own_g, *data)
    groups = [list(range(start, start + 2 * n_gen)) for start in range(0, n_gen * n_dat, 2 * n_gen)]
    totals = lax.all_to_all(col, ("dat", "gen"), 0, 0, axis_index_groups=groups, tiled=True)
    top = jnp.max(totals, axis=0)
    total = top + jnp.log2(jnp.sum(jnp.exp2(totals - top[None, :]), axis=0))
    new_data = own_g[0] - (EPS * LN2) * total + EPS * math.log(rows * n_gen / half)
    return f.reshape(rows), new_data


def solution(mesh):
    in_specs = (P(("gen", "dat"), None), P(("dat", "gen"), None), P(("dat", "gen")))
    out_specs = (P(("gen", "dat")), P(("dat", "gen")))
    return jax.shard_map(per_device, mesh=mesh, in_specs=in_specs, out_specs=out_specs, check_vma=False)
```

```python
import functools
import math

import jax
import jax.numpy as jnp
from jax import lax
from jax.experimental import pallas as pl
from jax.experimental.pallas import tpu as pltpu
from jax.sharding import PartitionSpec as P

EPS = 0.05
LOG2E = 1.4426950408889634
LN2 = 0.6931471805599453
SCALE = LOG2E / EPS
LANES = 128
TILE = 16
LIFT = 100.0
FLOOR = 2.0**-90
MIB = 1024 * 1024
NOTHING = -1e30


def round_up(value, step):
    return -(-value // step) * step


def swap(value, axis, mask):
    return lax.ppermute(value, axis, [(k, k ^ mask) for k in range(lax.axis_size(axis))])


def gather_gen(gen_own):
    gens = [(gen_own, 0)]
    bit = lax.axis_size("dat") // 2
    while bit > 1:
        gens += [(swap(array, "dat", bit), mask ^ bit) for array, mask in gens]
        bit //= 2
    return [array for array, _ in gens], [mask for _, mask in gens]


def gather_column(message, column):
    span = message.shape[0]
    far = range(2, lax.axis_size("gen"), 2)
    for k, mask in enumerate(far):
        column = lax.dynamic_update_slice(column, swap(message, "gen", mask), ((k + 1) * span, 0))
    return column, [0, *far]


def pack_kernel(y_ref, g_ref, packed_ref, column_ref):
    share, width = y_ref.shape
    tall = packed_ref.shape[0] - TILE
    y = y_ref[...]
    wide = y.astype(jnp.float32)
    sq = jnp.sum(wide * wide, axis=1, keepdims=True)
    sq = jnp.broadcast_to(sq, (share, LANES)).T[0:1, :]
    bias = SCALE * (g_ref[...] - sq / width)
    first = bias.astype(jnp.bfloat16).astype(jnp.float32)
    rest = bias - first
    second = rest.astype(jnp.bfloat16).astype(jnp.float32)
    third = rest - second
    row = lax.broadcasted_iota(jnp.int32, (TILE, share), 0)
    pieces = jnp.where(row == 0, first, jnp.where(row == 1, second, jnp.where(row == 2, third, 0.0)))
    if share < tall:
        packed_ref[...] = jnp.zeros(packed_ref.shape, jnp.bfloat16)
    else:
        packed_ref[tall:, :] = jnp.zeros((TILE, width), jnp.bfloat16)
    packed_ref[:share, :] = y
    packed_ref[tall:, :share] = pieces.astype(jnp.bfloat16)
    column_ref[: packed_ref.shape[0], :] = packed_ref[...]


def unpack(parts, share, y_ref, b_ref):
    tall = round_up(share, TILE)
    span = tall + TILE
    batch = TILE // math.gcd(share, TILE)
    held = []
    k = 0
    for part in parts:
        for start in range(0, part.shape[0], span):
            pieces = part[start + tall : start + span, :share].astype(jnp.float32)
            bias = pieces[0:1, :] + pieces[1:2, :] + pieces[2:3, :]
            b_ref[k * share : (k + 1) * share, :] = jnp.broadcast_to(bias, (LANES, share)).T
            if batch == 1:
                y_ref[k * share : (k + 1) * share, :] = part[start : start + share, :]
            else:
                held.append(part[start : start + tall, :].astype(jnp.float32)[:share, :])
                if len(held) == batch:
                    end = (k + 1) * share
                    y_ref[end - batch * share : end, :] = jnp.concatenate(held, axis=0).astype(jnp.bfloat16)
                    held = []
            k += 1


def norm_kernel(x_ref, sq_ref, copy_ref):
    copy_ref[...] = x_ref[...]
    x = x_ref[...].astype(jnp.float32)
    square = x * x
    high = square.astype(jnp.bfloat16)
    low = (square - high.astype(jnp.float32)).astype(jnp.bfloat16)
    ones = jnp.ones((TILE, x.shape[1]), jnp.bfloat16)
    sq = jnp.zeros((TILE, x.shape[0]), jnp.float32)
    for half in (high, low):
        sq += lax.dot_general(ones, half, (((1,), (1,)), ((), ())), preferred_element_type=jnp.float32)
    for k in range(sq_ref.shape[0]):
        sq_ref[k : k + 1, :] = sq[0:1, k * LANES : (k + 1) * LANES]


def spans(total, step):
    return [(start, min(step, total - start)) for start in range(0, total, step)]


def dots(y, x):
    return lax.dot_general(y, x, (((1,), (1,)), ((), ())), preferred_element_type=jnp.float32)


def across(values, count):
    return jnp.concatenate([values] * count, axis=1)


def each_pair(xs, block, dots_ref, fill, visit):
    rows = xs[0].shape[0]
    pair = 2 if rows // block % 2 == 0 else 1
    for place, x_ref in enumerate(xs):

        def step(index, carry, place=place, x_ref=x_ref):
            firsts = [(index * pair + k) * block for k in range(pair)]
            for k, first in enumerate(firsts):
                fill(dots_ref.at[k], x_ref[pl.ds(pl.multiple_of(first, block), block), :])
            for k, first in enumerate(firsts):
                visit(dots_ref.at[k], (place * rows + first) // LANES)
            return carry

        lax.fori_loop(0, rows // block // pair, step, 0)


def eight(values, op):
    groups = values.reshape(values.shape[0] // 8, 8, values.shape[1])
    return op(groups, axis=0)


def fold(values, op):
    out = values[:, :LANES]
    for start in range(LANES, values.shape[1], LANES):
        out = op(out, values[:, start : start + LANES])
    return out


def row_kernel(*refs, count, share, block, tall, merge):
    xs, refs = refs[:count], refs[count:]
    *parts, l_ref, y_ref, b_ref, t_ref = refs
    before = parts.pop() if merge else None
    unpack(parts, share, y_ref, b_ref)
    cols, width = y_ref.shape
    alpha = 2.0 * SCALE / width
    repeat = block // LANES

    def fill(slot, x):
        slot[...] = dots(y_ref[...], x)

    def visit(slot, place):
        top = None
        for start, size in spans(cols, tall):
            here = slice(start, start + size)
            t = alpha * slot[here, :] + across(b_ref[here, :], repeat)
            slot[here, :] = t
            part = eight(t, jnp.max)
            top = part if top is None else jnp.maximum(top, part)
        top = jnp.max(top, axis=0, keepdims=True)
        total = None
        for start, size in spans(cols, tall):
            part = eight(jnp.exp2(slot[start : start + size, :] - top), jnp.sum)
            total = part if total is None else total + part
        log_sum = top + jnp.log2(jnp.sum(total, axis=0, keepdims=True))
        for k in range(repeat):
            l_ref[pl.ds(place + k, 1), :] = log_sum[:, k * LANES : (k + 1) * LANES]

    each_pair(xs, block, t_ref, fill, visit)
    if merge:
        l_ref[...] = merged([before[...], l_ref[...]])


def merged(pieces):
    top = functools.reduce(jnp.maximum, pieces)
    return top + jnp.log2(sum(jnp.exp2(piece - top) for piece in pieces))


def column_kernel(*refs, count, share, block, tall, orders, masks, log_cols):
    xs, refs = refs[:count], refs[count:]
    logs, refs = refs[: len(orders)], refs[len(orders) :]
    sq_ref, g_ref, *data, f_ref, own_g_ref, col_ref, l_ref, sum_ref, top_ref, t_ref = refs
    ys, biases = data[::2], data[1::2]
    rows, width = xs[0].shape
    alpha = 2.0 * SCALE / width
    repeat = block // LANES
    tiles = rows // LANES
    for k in range(count):
        pieces = [log[order[k] * tiles : (order[k] + 1) * tiles, :] for log, order in zip(logs, orders)]
        l_ref[k * tiles : (k + 1) * tiles, :] = merged(pieces)
    own_g_ref[...] = g_ref[...]
    f_ref[...] = sq_ref[...] / width - (EPS * LN2) * l_ref[:tiles, :] + EPS * log_cols

    def fill(slot, x):
        offset = 0
        for y_ref in ys:
            cols = y_ref.shape[0]
            slot[offset : offset + cols, :] = dots(y_ref[...], x)
            offset += cols

    def each(lift, visit):
        def visit_all(slot, place):
            log_here = jnp.concatenate([l_ref[pl.ds(place + k, 1), :] for k in range(repeat)], axis=1) - lift
            offset = 0
            for b_ref in biases:
                for start, size in spans(b_ref.shape[0], tall):
                    here = slice(offset + start, offset + start + size)
                    bias = across(b_ref[start : start + size, :], repeat)
                    visit(here, alpha * slot[here, :] + bias - log_here)
                offset += b_ref.shape[0]

        each_pair(xs, block, t_ref, fill, visit_all)

    def add(here, values):
        sum_ref[here, :] += fold(jnp.exp2(values), jnp.add)

    def raise_top(here, values):
        top_ref[here, :] = jnp.maximum(top_ref[here, :], fold(values, jnp.maximum))

    def add_from_top(here, values):
        sum_ref[here, :] += fold(jnp.exp2(values - across(top_ref[here, :], repeat)), jnp.add)

    sum_ref[...] = jnp.zeros(sum_ref.shape, jnp.float32)
    each(LIFT, add)
    least = jnp.min(jnp.sum(sum_ref[...], axis=1, keepdims=True))
    top_ref[...] = jnp.full(top_ref.shape, -LIFT, jnp.float32)

    @pl.when(jnp.logical_not(least >= FLOOR))
    def _():
        top_ref[...] = jnp.full(top_ref.shape, -jnp.inf, jnp.float32)
        each(0.0, raise_top)
        top = jnp.max(top_ref[...], axis=1, keepdims=True)
        top_ref[...] = jnp.broadcast_to(top, top_ref.shape)
        sum_ref[...] = jnp.zeros(sum_ref.shape, jnp.float32)
        each(0.0, add_from_top)

    gen, dat = lax.axis_index("gen"), lax.axis_index("dat")
    n_gen = lax.axis_size("gen")
    col_ref[...] = jnp.full(col_ref.shape, NOTHING, jnp.float32)
    for k, mask in enumerate(masks):
        here = slice(k * share, (k + 1) * share)
        total = jnp.sum(sum_ref[here, :].T, axis=0, keepdims=True)
        place = (dat ^ mask[1]) * n_gen + (gen ^ mask[0])
        col_ref[pl.ds(place, 1), :] = top_ref[here, :].T[0:1, :] + jnp.log2(total)


def per_device(gen_samples, data_samples, data_potential):
    rows, width = gen_samples.shape
    n_gen, n_dat = lax.axis_size("gen"), lax.axis_size("dat")
    share = data_samples.shape[0]
    half = share * n_gen
    cols = 2 * half
    tiles = rows // LANES
    span = round_up(share, TILE) + TILE
    own_g = data_potential.reshape(1, share)
    message, column = pl.pallas_call(
        pack_kernel,
        out_shape=(
            jax.ShapeDtypeStruct((span, width), jnp.bfloat16),
            jax.ShapeDtypeStruct((span * (n_gen // 2), width), jnp.bfloat16),
        ),
        compiler_params=pltpu.CompilerParams(vmem_limit_bytes=4 * MIB),
    )(data_samples, own_g)
    xs, order = gather_gen(gen_samples)
    column, far = gather_column(message, column)
    sq, xs[0] = pl.pallas_call(
        norm_kernel,
        out_shape=(
            jax.ShapeDtypeStruct((tiles, LANES), jnp.float32),
            jax.ShapeDtypeStruct(gen_samples.shape, gen_samples.dtype),
        ),
        compiler_params=pltpu.CompilerParams(vmem_limit_bytes=8 * MIB),
    )(gen_samples)
    block = min(256, rows)
    tall = 64
    pair = 2 if rows // block % 2 == 0 else 1

    def cost(count):
        return pl.CostEstimate(
            flops=2 * rows * len(xs) * count * width,
            bytes_accessed=2 * (rows * len(xs) + count) * width,
            transcendentals=rows * len(xs) * count,
        )

    def row_pass(parts, before):
        count = len(parts) * half // 2
        return pl.pallas_call(
            functools.partial(
                row_kernel, count=len(xs), share=share, block=block, tall=tall, merge=bool(before)
            ),
            out_shape=(
                jax.ShapeDtypeStruct((len(xs) * tiles, LANES), jnp.float32),
                jax.ShapeDtypeStruct((count, width), jnp.bfloat16),
                jax.ShapeDtypeStruct((count, LANES), jnp.float32),
            ),
            scratch_shapes=[pltpu.VMEM((pair, count, block), jnp.float32)],
            compiler_params=pltpu.CompilerParams(vmem_limit_bytes=12 * MIB),
            cost_estimate=cost(count),
        )(*xs, *parts, *before)

    near = swap(column, "gen", 1)
    twin = swap(column, "dat", 1)
    log, *data = row_pass([column, twin], [])
    near, log = lax.optimization_barrier((near, log))
    near_twin = swap(near, "dat", 1)
    log, *more = row_pass([near], [log])
    data += more
    near_twin, log = lax.optimization_barrier((near_twin, log))
    log, *more = row_pass([near_twin], [log])
    data += more
    masks = [(g ^ a, b) for a in (0, 1) for b in (0, 1) for g in far]
    logs = [log]
    logs += [swap(logs[0], "dat", m) for m in order[1:]]
    orders = [[order.index(m ^ partner) for m in order] for partner in order]
    f, own_g, col = pl.pallas_call(
        functools.partial(
            column_kernel,
            count=len(xs),
            share=share,
            block=block,
            tall=tall,
            orders=orders,
            masks=masks,
            log_cols=math.log(half * n_dat),
        ),
        out_shape=(
            jax.ShapeDtypeStruct((tiles, LANES), jnp.float32),
            jax.ShapeDtypeStruct((1, share), jnp.float32),
            jax.ShapeDtypeStruct((n_dat * n_gen, share), jnp.float32),
        ),
        scratch_shapes=[
            pltpu.VMEM((len(xs) * tiles, LANES), jnp.float32),
            pltpu.VMEM((cols, LANES), jnp.float32),
            pltpu.VMEM((cols, LANES), jnp.float32),
            pltpu.VMEM((pair, cols, block), jnp.float32),
        ],
        compiler_params=pltpu.CompilerParams(vmem_limit_bytes=16 * MIB),
        cost_estimate=cost(cols),
    )(*xs, *logs, sq, own_g, *data)
    totals = lax.all_to_all(col, ("dat", "gen"), 0, 0, tiled=True)
    top = jnp.max(totals, axis=0)
    total = top + jnp.log2(jnp.sum(jnp.exp2(totals - top[None, :]), axis=0))
    new_data = own_g[0] - (EPS * LN2) * total + EPS * math.log(rows * n_gen / half)
    return f.reshape(rows), new_data


def solution(mesh):
    in_specs = (P(("gen", "dat"), None), P(("dat", "gen"), None), P(("dat", "gen")))
    out_specs = (P(("gen", "dat")), P(("dat", "gen")))
    return jax.shard_map(per_device, mesh=mesh, in_specs=in_specs, out_specs=out_specs, check_vma=False)
```

```python
import functools
import math

import jax
import jax.numpy as jnp
from jax import lax
from jax.experimental import pallas as pl
from jax.experimental.pallas import tpu as pltpu
from jax.sharding import PartitionSpec as P

EPS = 0.05
LOG2E = 1.4426950408889634
LN2 = 0.6931471805599453
SCALE = LOG2E / EPS
LANES = 128
TILE = 16
LIFT = 100.0
FLOOR = 2.0**-90
MIB = 1024 * 1024
NOTHING = -1e30


def round_up(value, step):
    return -(-value // step) * step


def swap(value, axis, mask):
    return lax.ppermute(value, axis, [(k, k ^ mask) for k in range(lax.axis_size(axis))])


def gather_gen(gen_own):
    gens = [(gen_own, 0)]
    bit = lax.axis_size("dat") // 2
    while bit > 1:
        gens += [(swap(array, "dat", bit), mask ^ bit) for array, mask in gens]
        bit //= 2
    return [array for array, _ in gens], [mask for _, mask in gens]


def gather_column(message, column):
    span = message.shape[0]
    far = range(2, lax.axis_size("gen"), 2)
    for k, mask in enumerate(far):
        column = lax.dynamic_update_slice(column, swap(message, "gen", mask), ((k + 1) * span, 0))
    return column, [0, *far]


def pack_kernel(y_hbm_ref, g_hbm_ref, packed_ref, column_ref, y_ref, g_ref, sems):
    copies = [
        pltpu.make_async_copy(y_hbm_ref, y_ref, sems.at[0]),
        pltpu.make_async_copy(g_hbm_ref, g_ref, sems.at[1]),
    ]
    for copy in copies:
        copy.start()
    for copy in copies:
        copy.wait()
    share, width = y_ref.shape
    tall = packed_ref.shape[0] - TILE
    y = y_ref[...]
    wide = y.astype(jnp.float32)
    sq = jnp.sum(wide * wide, axis=1, keepdims=True)
    sq = jnp.broadcast_to(sq, (share, LANES)).T[0:1, :]
    bias = SCALE * (g_ref[...] - sq / width)
    first = bias.astype(jnp.bfloat16).astype(jnp.float32)
    rest = bias - first
    second = rest.astype(jnp.bfloat16).astype(jnp.float32)
    third = rest - second
    row = lax.broadcasted_iota(jnp.int32, (TILE, share), 0)
    pieces = jnp.where(row == 0, first, jnp.where(row == 1, second, jnp.where(row == 2, third, 0.0)))
    if share < tall:
        packed_ref[...] = jnp.zeros(packed_ref.shape, jnp.bfloat16)
    else:
        packed_ref[tall:, :] = jnp.zeros((TILE, width), jnp.bfloat16)
    packed_ref[:share, :] = y
    packed_ref[tall:, :share] = pieces.astype(jnp.bfloat16)
    column_ref[: packed_ref.shape[0], :] = packed_ref[...]


def unpack(parts, share, y_ref, b_ref):
    tall = round_up(share, TILE)
    span = tall + TILE
    batch = TILE // math.gcd(share, TILE)
    held = []
    k = 0
    for part in parts:
        for start in range(0, part.shape[0], span):
            pieces = part[start + tall : start + span, :share].astype(jnp.float32)
            bias = pieces[0:1, :] + pieces[1:2, :] + pieces[2:3, :]
            b_ref[k * share : (k + 1) * share, :] = jnp.broadcast_to(bias, (LANES, share)).T
            if batch == 1:
                y_ref[k * share : (k + 1) * share, :] = part[start : start + share, :]
            else:
                held.append(part[start : start + tall, :].astype(jnp.float32)[:share, :])
                if len(held) == batch:
                    end = (k + 1) * share
                    y_ref[end - batch * share : end, :] = jnp.concatenate(held, axis=0).astype(jnp.bfloat16)
                    held = []
            k += 1


def norm_kernel(x_ref, sq_ref, copy_ref):
    copy_ref[...] = x_ref[...]
    x = x_ref[...].astype(jnp.float32)
    square = x * x
    high = square.astype(jnp.bfloat16)
    low = (square - high.astype(jnp.float32)).astype(jnp.bfloat16)
    ones = jnp.ones((TILE, x.shape[1]), jnp.bfloat16)
    sq = jnp.zeros((TILE, x.shape[0]), jnp.float32)
    for half in (high, low):
        sq += lax.dot_general(ones, half, (((1,), (1,)), ((), ())), preferred_element_type=jnp.float32)
    for k in range(sq_ref.shape[0]):
        sq_ref[k : k + 1, :] = sq[0:1, k * LANES : (k + 1) * LANES]


def spans(total, step):
    return [(start, min(step, total - start)) for start in range(0, total, step)]


def dots(y, x):
    return lax.dot_general(y, x, (((1,), (1,)), ((), ())), preferred_element_type=jnp.float32)


def across(values, count):
    return jnp.concatenate([values] * count, axis=1)


def each_pair(xs, dots_ref, fill, visit):
    rows = xs[0].shape[0]
    half = rows // 2
    for place, x_ref in enumerate(xs):
        for k in range(2):
            fill(dots_ref.at[k], x_ref[k * half : (k + 1) * half, :])
        for k in range(2):
            visit(dots_ref.at[k], (place * rows + k * half) // LANES)


def eight(values, op):
    groups = values.reshape(values.shape[0] // 8, 8, values.shape[1])
    return op(groups, axis=0)


def fold(values, op):
    out = values[:, :LANES]
    for start in range(LANES, values.shape[1], LANES):
        out = op(out, values[:, start : start + LANES])
    return out


def row_kernel(*refs, count, share, tall, merge):
    xs, refs = refs[:count], refs[count:]
    *parts, l_ref, y_ref, b_ref, t_ref = refs
    before = parts.pop() if merge else None
    unpack(parts, share, y_ref, b_ref)
    cols, width = y_ref.shape
    alpha = 2.0 * SCALE / width
    repeat = t_ref.shape[2] // LANES

    def fill(slot, x):
        slot[...] = dots(y_ref[...], x)

    def visit(slot, place):
        top = None
        for start, size in spans(cols, tall):
            here = slice(start, start + size)
            t = alpha * slot[here, :] + across(b_ref[here, :], repeat)
            slot[here, :] = t
            part = eight(t, jnp.max)
            top = part if top is None else jnp.maximum(top, part)
        top = jnp.max(top, axis=0, keepdims=True)
        total = None
        for start, size in spans(cols, tall):
            part = eight(jnp.exp2(slot[start : start + size, :] - top), jnp.sum)
            total = part if total is None else total + part
        log_sum = top + jnp.log2(jnp.sum(total, axis=0, keepdims=True))
        for k in range(repeat):
            l_ref[pl.ds(place + k, 1), :] = log_sum[:, k * LANES : (k + 1) * LANES]

    each_pair(xs, t_ref, fill, visit)
    if merge:
        l_ref[...] = merged([before[...], l_ref[...]])


def merged(pieces):
    top = functools.reduce(jnp.maximum, pieces)
    return top + jnp.log2(sum(jnp.exp2(piece - top) for piece in pieces))


def column_kernel(*refs, count, share, tall, orders, masks, log_cols):
    xs, refs = refs[:count], refs[count:]
    logs, refs = refs[: len(orders)], refs[len(orders) :]
    sq_ref, g_ref, *data, f_ref, own_g_ref, col_ref, l_ref, sum_ref, top_ref, t_ref = refs
    ys, biases = data[::2], data[1::2]
    rows, width = xs[0].shape
    alpha = 2.0 * SCALE / width
    repeat = t_ref.shape[2] // LANES
    tiles = f_ref.shape[0]
    for k in range(len(orders)):
        pieces = [log[order[k] * tiles : (order[k] + 1) * tiles, :] for log, order in zip(logs, orders)]
        l_ref[k * tiles : (k + 1) * tiles, :] = merged(pieces)
    own_g_ref[...] = g_ref[...]
    f_ref[...] = sq_ref[...] / width - (EPS * LN2) * l_ref[:tiles, :] + EPS * log_cols

    def fill(slot, x):
        offset = 0
        for y_ref in ys:
            cols = y_ref.shape[0]
            slot[offset : offset + cols, :] = dots(y_ref[...], x)
            offset += cols

    def each(lift, visit):
        def visit_all(slot, place):
            log_here = jnp.concatenate([l_ref[pl.ds(place + k, 1), :] for k in range(repeat)], axis=1) - lift
            offset = 0
            for b_ref in biases:
                for start, size in spans(b_ref.shape[0], tall):
                    here = slice(offset + start, offset + start + size)
                    bias = across(b_ref[start : start + size, :], repeat)
                    visit(here, alpha * slot[here, :] + bias - log_here)
                offset += b_ref.shape[0]

        each_pair(xs, t_ref, fill, visit_all)

    def add(here, values):
        sum_ref[here, :] += fold(jnp.exp2(values), jnp.add)

    def raise_top(here, values):
        top_ref[here, :] = jnp.maximum(top_ref[here, :], fold(values, jnp.maximum))

    def add_from_top(here, values):
        sum_ref[here, :] += fold(jnp.exp2(values - across(top_ref[here, :], repeat)), jnp.add)

    sum_ref[...] = jnp.zeros(sum_ref.shape, jnp.float32)
    each(LIFT, add)
    least = jnp.min(jnp.sum(sum_ref[...], axis=1, keepdims=True))
    top_ref[...] = jnp.full(top_ref.shape, -LIFT, jnp.float32)

    @pl.when(jnp.logical_not(least >= FLOOR))
    def _():
        top_ref[...] = jnp.full(top_ref.shape, -jnp.inf, jnp.float32)
        each(0.0, raise_top)
        top = jnp.max(top_ref[...], axis=1, keepdims=True)
        top_ref[...] = jnp.broadcast_to(top, top_ref.shape)
        sum_ref[...] = jnp.zeros(sum_ref.shape, jnp.float32)
        each(0.0, add_from_top)

    gen, dat = lax.axis_index("gen"), lax.axis_index("dat")
    n_gen = lax.axis_size("gen")
    col_ref[...] = jnp.full(col_ref.shape, NOTHING, jnp.float32)
    for k, mask in enumerate(masks):
        here = slice(k * share, (k + 1) * share)
        total = jnp.sum(sum_ref[here, :].T, axis=0, keepdims=True)
        place = (dat ^ mask[1]) * n_gen + (gen ^ mask[0])
        col_ref[pl.ds(place, 1), :] = top_ref[here, :].T[0:1, :] + jnp.log2(total)


def per_device(gen_samples, data_samples, data_potential):
    rows, width = gen_samples.shape
    n_gen, n_dat = lax.axis_size("gen"), lax.axis_size("dat")
    share = data_samples.shape[0]
    half = share * n_gen
    cols = 2 * half
    tiles = rows // LANES
    span = round_up(share, TILE) + TILE
    own_g = data_potential.reshape(1, share)
    message, column = pl.pallas_call(
        pack_kernel,
        out_shape=(
            jax.ShapeDtypeStruct((span, width), jnp.bfloat16),
            jax.ShapeDtypeStruct((span * (n_gen // 2), width), jnp.bfloat16),
        ),
        in_specs=[pl.BlockSpec(memory_space=pltpu.HBM)] * 2,
        scratch_shapes=[
            pltpu.VMEM((share, width), jnp.bfloat16),
            pltpu.VMEM((1, share), jnp.float32),
            pltpu.SemaphoreType.DMA((2,)),
        ],
        compiler_params=pltpu.CompilerParams(vmem_limit_bytes=4 * MIB),
    )(*[pltpu.with_memory_space_constraint(array, pltpu.HBM) for array in (data_samples, own_g)])
    xs, order = gather_gen(gen_samples)
    column, far = gather_column(message, column)
    sq, xs[0] = pl.pallas_call(
        norm_kernel,
        out_shape=(
            jax.ShapeDtypeStruct((tiles, LANES), jnp.float32),
            jax.ShapeDtypeStruct((rows, width), gen_samples.dtype),
        ),
        compiler_params=pltpu.CompilerParams(vmem_limit_bytes=8 * MIB),
    )(gen_samples)
    tall = 64

    def cost(count):
        return pl.CostEstimate(
            flops=2 * rows * len(xs) * count * width,
            bytes_accessed=2 * (rows * len(xs) + count) * width,
            transcendentals=rows * len(xs) * count,
        )

    def row_pass(parts, before):
        count = len(parts) * half // 2
        return pl.pallas_call(
            functools.partial(
                row_kernel, count=len(xs), share=share, tall=tall, merge=bool(before)
            ),
            out_shape=(
                jax.ShapeDtypeStruct((len(order) * tiles, LANES), jnp.float32),
                jax.ShapeDtypeStruct((count, width), jnp.bfloat16),
                jax.ShapeDtypeStruct((count, LANES), jnp.float32),
            ),
            scratch_shapes=[pltpu.VMEM((2, count, rows // 2), jnp.float32)],
            compiler_params=pltpu.CompilerParams(vmem_limit_bytes=12 * MIB),
            cost_estimate=cost(count),
        )(*xs, *parts, *before)

    near = swap(column, "gen", 1)
    xs[1:], held = lax.optimization_barrier((xs[1:], column))
    twin = swap(held, "dat", 1)
    log, *data = row_pass([column], [])
    twin, log = lax.optimization_barrier((twin, log))
    log, *more = row_pass([twin], [log])
    data += more
    near, log = lax.optimization_barrier((near, log))
    near_twin = swap(near, "dat", 1)
    log, *more = row_pass([near], [log])
    data += more
    near_twin, log = lax.optimization_barrier((near_twin, log))
    log, *more = row_pass([near_twin], [log])
    data += more
    masks = [(g ^ a, b) for a in (0, 1) for b in (0, 1) for g in far]
    logs = [log]
    logs += [swap(logs[0], "dat", m) for m in order[1:]]
    orders = [[order.index(m ^ partner) for m in order] for partner in order]
    f, own_g, col = pl.pallas_call(
        functools.partial(
            column_kernel,
            count=len(xs),
            share=share,
            tall=tall,
            orders=orders,
            masks=masks,
            log_cols=math.log(half * n_dat),
        ),
        out_shape=(
            jax.ShapeDtypeStruct((tiles, LANES), jnp.float32),
            jax.ShapeDtypeStruct((1, share), jnp.float32),
            jax.ShapeDtypeStruct((n_dat * n_gen, share), jnp.float32),
        ),
        scratch_shapes=[
            pltpu.VMEM((len(order) * tiles, LANES), jnp.float32),
            pltpu.VMEM((cols, LANES), jnp.float32),
            pltpu.VMEM((cols, LANES), jnp.float32),
            pltpu.VMEM((2, cols, rows // 2), jnp.float32),
        ],
        compiler_params=pltpu.CompilerParams(vmem_limit_bytes=16 * MIB),
        cost_estimate=cost(cols),
    )(*xs, *logs, sq, own_g, *data)
    totals = lax.all_to_all(col, ("dat", "gen"), 0, 0, tiled=True)
    top = jnp.max(totals, axis=0)
    total = top + jnp.log2(jnp.sum(jnp.exp2(totals - top[None, :]), axis=0))
    new_data = own_g[0] - (EPS * LN2) * total + EPS * math.log(rows * n_gen / half)
    return f.reshape(rows), new_data


def solution(mesh):
    in_specs = (P(("gen", "dat"), None), P(("dat", "gen"), None), P(("dat", "gen")))
    out_specs = (P(("gen", "dat")), P(("dat", "gen")))
    return jax.shard_map(per_device, mesh=mesh, in_specs=in_specs, out_specs=out_specs, check_vma=False)
```

```python
import functools
import math

import jax
import jax.numpy as jnp
from jax import lax
from jax.experimental import pallas as pl
from jax.experimental.pallas import tpu as pltpu
from jax.sharding import PartitionSpec as P

EPS = 0.05
LOG2E = 1.4426950408889634
LN2 = 0.6931471805599453
SCALE = LOG2E / EPS
LANES = 128
TILE = 16
LIFT = 50.0
FLOOR = 2.0**-41
MIB = 1024 * 1024
NOTHING = -1e30


def round_up(value, step):
    return -(-value // step) * step


def swap(value, axis, mask):
    return lax.ppermute(value, axis, [(k, k ^ mask) for k in range(lax.axis_size(axis))])


def gather_gen(gen_own):
    gens = [(gen_own, 0)]
    bit = lax.axis_size("dat") // 2
    while bit > 1:
        gens += [(swap(array, "dat", bit), mask ^ bit) for array, mask in gens]
        bit //= 2
    return [array for array, _ in gens], [mask for _, mask in gens]


def gather_column(message, column):
    span = message.shape[0]
    far = range(2, lax.axis_size("gen"), 2)
    for k, mask in enumerate(far):
        column = lax.dynamic_update_slice(column, swap(message, "gen", mask), ((k + 1) * span, 0))
    return column, [0, *far]


def pack_kernel(y_hbm_ref, g_hbm_ref, packed_ref, column_ref, own_g_ref, y_ref, g_ref, sems):
    copies = [
        pltpu.make_async_copy(y_hbm_ref, y_ref, sems.at[0]),
        pltpu.make_async_copy(g_hbm_ref, g_ref, sems.at[1]),
    ]
    for copy in copies:
        copy.start()
    for copy in copies:
        copy.wait()
    share, width = y_ref.shape
    tall = packed_ref.shape[0] - TILE
    own_g_ref[...] = g_ref[...]
    y = y_ref[...]
    wide = y.astype(jnp.float32)
    sq = jnp.sum(wide * wide, axis=1, keepdims=True)
    sq = jnp.broadcast_to(sq, (share, LANES)).T[0:1, :]
    bias = SCALE * (g_ref[...] - sq / width)
    first = bias.astype(jnp.bfloat16).astype(jnp.float32)
    rest = bias - first
    second = rest.astype(jnp.bfloat16).astype(jnp.float32)
    third = rest - second
    row = lax.broadcasted_iota(jnp.int32, (TILE, share), 0)
    pieces = jnp.where(row == 0, first, jnp.where(row == 1, second, jnp.where(row == 2, third, 0.0)))
    if share < tall:
        packed_ref[...] = jnp.zeros(packed_ref.shape, jnp.bfloat16)
    else:
        packed_ref[tall:, :] = jnp.zeros((TILE, width), jnp.bfloat16)
    packed_ref[:share, :] = y
    packed_ref[tall:, :share] = pieces.astype(jnp.bfloat16)
    column_ref[: packed_ref.shape[0], :] = packed_ref[...]


def unpack(parts, share, y_ref, b_ref):
    tall = round_up(share, TILE)
    span = tall + TILE
    batch = TILE // math.gcd(share, TILE)
    held = []
    k = 0
    for part in parts:
        for start in range(0, part.shape[0], span):
            pieces = part[start + tall : start + span, :share].astype(jnp.float32)
            bias = pieces[0:1, :] + pieces[1:2, :] + pieces[2:3, :]
            b_ref[k * share : (k + 1) * share, :] = jnp.broadcast_to(bias, (LANES, share)).T
            if batch == 1:
                y_ref[k * share : (k + 1) * share, :] = part[start : start + share, :]
            else:
                held.append(part[start : start + tall, :].astype(jnp.float32)[:share, :])
                if len(held) == batch:
                    end = (k + 1) * share
                    y_ref[end - batch * share : end, :] = jnp.concatenate(held, axis=0).astype(jnp.bfloat16)
                    held = []
            k += 1


def norm_kernel(x_ref, sq_ref, copy_ref):
    copy_ref[...] = x_ref[...]
    x = x_ref[...].astype(jnp.float32)
    square = x * x
    high = square.astype(jnp.bfloat16)
    low = (square - high.astype(jnp.float32)).astype(jnp.bfloat16)
    ones = jnp.ones((TILE, x.shape[1]), jnp.bfloat16)
    sq = jnp.zeros((TILE, x.shape[0]), jnp.float32)
    for half in (high, low):
        sq += lax.dot_general(ones, half, (((1,), (1,)), ((), ())), preferred_element_type=jnp.float32)
    for k in range(sq_ref.shape[0]):
        sq_ref[k : k + 1, :] = sq[0:1, k * LANES : (k + 1) * LANES]


def spans(total, step):
    return [(start, min(step, total - start)) for start in range(0, total, step)]


def dots(y, x):
    return lax.dot_general(y, x, (((1,), (1,)), ((), ())), preferred_element_type=jnp.float32)


def across(values, count):
    return jnp.concatenate([values] * count, axis=1)


def each_pair(xs, dots_ref, fill, visit):
    rows = xs[0].shape[0]
    half = rows // 2
    for place, x_ref in enumerate(xs):
        for k in range(2):
            fill(dots_ref.at[k], x_ref[k * half : (k + 1) * half, :])
        for k in range(2):
            visit(dots_ref.at[k], (place * rows + k * half) // LANES)


def eight(values, op):
    groups = values.reshape(values.shape[0] // 8, 8, values.shape[1])
    return op(groups, axis=0)


def fold(values, op):
    out = values[:, :LANES]
    for start in range(LANES, values.shape[1], LANES):
        out = op(out, values[:, start : start + LANES])
    return out


def row_kernel(*refs, count, share, tall, merge):
    xs, refs = refs[:count], refs[count:]
    *parts, l_ref, top_ref, e_ref, y_ref, b_ref, t_ref = refs
    before = parts.pop() if merge else None
    unpack(parts, share, y_ref, b_ref)
    cols, width = y_ref.shape
    alpha = 2.0 * SCALE / width
    repeat = t_ref.shape[2] // LANES

    def fill(slot, x):
        slot[...] = dots(y_ref[...], x)

    def visit(slot, place):
        top = None
        for start, size in spans(cols, tall):
            here = slice(start, start + size)
            t = alpha * slot[here, :] + across(b_ref[here, :], repeat)
            slot[here, :] = t
            part = eight(t, jnp.max)
            top = part if top is None else jnp.maximum(top, part)
        base = jnp.max(top, axis=0, keepdims=True) - LIFT
        total = None
        for start, size in spans(cols, tall):
            here = slice(start, start + size)
            e = jnp.exp2(slot[here, :] - base)
            e_ref[place // repeat, here, :] = e
            part = eight(e, jnp.sum)
            total = part if total is None else total + part
        log_sum = base + jnp.log2(jnp.sum(total, axis=0, keepdims=True))
        for k in range(repeat):
            lanes = slice(k * LANES, (k + 1) * LANES)
            l_ref[place + k : place + k + 1, :] = log_sum[:, lanes]
            top_ref[place + k : place + k + 1, :] = base[:, lanes] + LIFT

    each_pair(xs, t_ref, fill, visit)
    if merge:
        l_ref[...] = merged([before[...], l_ref[...]])


def merged(pieces):
    top = functools.reduce(jnp.maximum, pieces)
    return top + jnp.log2(sum(jnp.exp2(piece - top) for piece in pieces))


def column_kernel(*refs, count, share, tall, orders, masks, log_cols):
    xs, refs = refs[:count], refs[count:]
    logs, refs = refs[: len(orders)], refs[len(orders) :]
    sq_ref, *data, f_ref, col_ref, l_ref, sum_ref, top_ref, t_ref = refs
    tops, es, ys, biases = data[::4], data[1::4], data[2::4], data[3::4]
    rows, width = xs[0].shape
    alpha = 2.0 * SCALE / width
    repeat = t_ref.shape[2] // LANES
    tiles = f_ref.shape[0]
    for k in range(len(orders)):
        pieces = [log[order[k] * tiles : (order[k] + 1) * tiles, :] for log, order in zip(logs, orders)]
        l_ref[k * tiles : (k + 1) * tiles, :] = merged(pieces)
    f_ref[...] = sq_ref[...] / width - (EPS * LN2) * l_ref[:tiles, :] + EPS * log_cols

    def fill(slot, x):
        offset = 0
        for y_ref in ys:
            cols = y_ref.shape[0]
            slot[offset : offset + cols, :] = dots(y_ref[...], x)
            offset += cols

    def each(visit):
        def visit_all(slot, place):
            log_here = jnp.concatenate([l_ref[place + k : place + k + 1, :] for k in range(repeat)], axis=1)
            offset = 0
            for b_ref in biases:
                for start, size in spans(b_ref.shape[0], tall):
                    here = slice(offset + start, offset + start + size)
                    bias = across(b_ref[start : start + size, :], repeat)
                    visit(here, alpha * slot[here, :] + bias - log_here)
                offset += b_ref.shape[0]

        each_pair(xs, t_ref, fill, visit_all)

    def raise_top(here, values):
        top_ref[here, :] = jnp.maximum(top_ref[here, :], fold(values, jnp.maximum))

    def add_from_top(here, values):
        sum_ref[here, :] += fold(jnp.exp2(values - across(top_ref[here, :], repeat)), jnp.add)

    offset = 0
    for held_ref, e_ref in zip(tops, es):
        weights = jnp.exp2(held_ref[...] - l_ref[...] + LIFT)
        scale = [
            jnp.concatenate([weights[k * repeat + i : k * repeat + i + 1, :] for i in range(repeat)], axis=1)
            for k in range(e_ref.shape[0])
        ]

        def add(index, carry, e_ref=e_ref, scale=scale, offset=offset):
            start = pl.multiple_of(index * tall, tall)
            here = pl.ds(start, tall)
            parts = [fold(e_ref[k, here, :] * scale[k], jnp.add) for k in range(len(scale))]
            sum_ref[pl.ds(offset + start, tall), :] = functools.reduce(jnp.add, parts)
            return carry

        lax.fori_loop(0, e_ref.shape[1] // tall, add, 0)
        offset += e_ref.shape[1]
    least = jnp.min(jnp.sum(sum_ref[...], axis=1, keepdims=True))
    top_ref[...] = jnp.full(top_ref.shape, -2.0 * LIFT, jnp.float32)

    @pl.when(jnp.logical_not(least >= FLOOR))
    def _():
        top_ref[...] = jnp.full(top_ref.shape, -jnp.inf, jnp.float32)
        each(raise_top)
        top = jnp.max(top_ref[...], axis=1, keepdims=True)
        top_ref[...] = jnp.broadcast_to(top, top_ref.shape)
        sum_ref[...] = jnp.zeros(sum_ref.shape, jnp.float32)
        each(add_from_top)

    gen, dat = lax.axis_index("gen"), lax.axis_index("dat")
    n_gen = lax.axis_size("gen")
    col_ref[...] = jnp.full(col_ref.shape, NOTHING, jnp.float32)
    for k, mask in enumerate(masks):
        here = slice(k * share, (k + 1) * share)
        total = jnp.sum(sum_ref[here, :].T, axis=0, keepdims=True)
        place = (dat ^ mask[1]) * n_gen + (gen ^ mask[0])
        col_ref[pl.ds(place, 1), :] = top_ref[here, :].T[0:1, :] + jnp.log2(total)


def per_device(gen_samples, data_samples, data_potential):
    rows, width = gen_samples.shape
    n_gen, n_dat = lax.axis_size("gen"), lax.axis_size("dat")
    share = data_samples.shape[0]
    half = share * n_gen
    cols = 2 * half
    tiles = rows // LANES
    span = round_up(share, TILE) + TILE
    own_g = data_potential.reshape(1, share)
    message, column, held_g = pl.pallas_call(
        pack_kernel,
        out_shape=(
            jax.ShapeDtypeStruct((span, width), jnp.bfloat16),
            jax.ShapeDtypeStruct((span * (n_gen // 2), width), jnp.bfloat16),
            jax.ShapeDtypeStruct((1, share), jnp.float32),
        ),
        in_specs=[pl.BlockSpec(memory_space=pltpu.HBM)] * 2,
        scratch_shapes=[
            pltpu.VMEM((share, width), jnp.bfloat16),
            pltpu.VMEM((1, share), jnp.float32),
            pltpu.SemaphoreType.DMA((2,)),
        ],
        compiler_params=pltpu.CompilerParams(vmem_limit_bytes=4 * MIB),
    )(*[pltpu.with_memory_space_constraint(array, pltpu.HBM) for array in (data_samples, own_g)])
    xs, order = gather_gen(gen_samples)
    column, far = gather_column(message, column)
    sq, xs[0] = pl.pallas_call(
        norm_kernel,
        out_shape=(
            jax.ShapeDtypeStruct((tiles, LANES), jnp.float32),
            jax.ShapeDtypeStruct((rows, width), gen_samples.dtype),
        ),
        compiler_params=pltpu.CompilerParams(vmem_limit_bytes=8 * MIB),
    )(gen_samples)
    tall = 64

    def cost(count):
        return pl.CostEstimate(
            flops=2 * rows * len(xs) * count * width,
            bytes_accessed=2 * (rows * len(xs) + count) * width,
            transcendentals=rows * len(xs) * count,
        )

    def row_pass(parts, before):
        count = len(parts) * half // 2
        return pl.pallas_call(
            functools.partial(
                row_kernel, count=len(xs), share=share, tall=tall, merge=bool(before)
            ),
            out_shape=(
                jax.ShapeDtypeStruct((len(order) * tiles, LANES), jnp.float32),
                jax.ShapeDtypeStruct((len(order) * tiles, LANES), jnp.float32),
                jax.ShapeDtypeStruct((2 * len(xs), count, rows // 2), jnp.float32),
                jax.ShapeDtypeStruct((count, width), jnp.bfloat16),
                jax.ShapeDtypeStruct((count, LANES), jnp.float32),
            ),
            scratch_shapes=[pltpu.VMEM((2, count, rows // 2), jnp.float32)],
            compiler_params=pltpu.CompilerParams(vmem_limit_bytes=12 * MIB),
            cost_estimate=cost(count),
        )(*xs, *parts, *before)

    near = swap(column, "gen", 1)
    xs[1:], held = lax.optimization_barrier((xs[1:], column))
    twin = swap(held, "dat", 1)
    log, *data = row_pass([column], [])
    near, log = lax.optimization_barrier((near, log))
    near_twin = swap(near, "dat", 1)
    log, *more = row_pass([near], [log])
    data += more
    twin, log = lax.optimization_barrier((twin, log))
    log, *more = row_pass([twin], [log])
    data += more
    near_twin, log = lax.optimization_barrier((near_twin, log))
    log, *more = row_pass([near_twin], [log])
    data += more
    masks = [(g ^ a, b) for b in (0, 1) for a in (0, 1) for g in far]
    logs = [log]
    logs += [swap(logs[0], "dat", m) for m in order[1:]]
    orders = [[order.index(m ^ partner) for m in order] for partner in order]
    f, col = pl.pallas_call(
        functools.partial(
            column_kernel,
            count=len(xs),
            share=share,
            tall=tall,
            orders=orders,
            masks=masks,
            log_cols=math.log(half * n_dat),
        ),
        out_shape=(
            jax.ShapeDtypeStruct((tiles, LANES), jnp.float32),
            jax.ShapeDtypeStruct((n_dat * n_gen, share), jnp.float32),
        ),
        scratch_shapes=[
            pltpu.VMEM((len(order) * tiles, LANES), jnp.float32),
            pltpu.VMEM((cols, LANES), jnp.float32),
            pltpu.VMEM((cols, LANES), jnp.float32),
            pltpu.VMEM((2, cols, rows // 2), jnp.float32),
        ],
        compiler_params=pltpu.CompilerParams(vmem_limit_bytes=16 * MIB),
        cost_estimate=cost(cols),
    )(*xs, *logs, sq, *data)
    totals = lax.all_to_all(col, ("dat", "gen"), 0, 0, tiled=True)
    top = jnp.max(totals, axis=0)
    total = top + jnp.log2(jnp.sum(jnp.exp2(totals - top[None, :]), axis=0))
    new_data = held_g[0] - (EPS * LN2) * total + EPS * math.log(rows * n_gen / half)
    return f.reshape(rows), new_data


def solution(mesh):
    in_specs = (P(("gen", "dat"), None), P(("dat", "gen"), None), P(("dat", "gen")))
    out_specs = (P(("gen", "dat")), P(("dat", "gen")))
    return jax.shard_map(per_device, mesh=mesh, in_specs=in_specs, out_specs=out_specs, check_vma=False)
```

```python
import functools
import math

import jax
import jax.numpy as jnp
from jax import lax
from jax.experimental import pallas as pl
from jax.experimental.pallas import tpu as pltpu
from jax.sharding import PartitionSpec as P

EPS = 0.05
LOG2E = 1.4426950408889634
LN2 = 0.6931471805599453
SCALE = LOG2E / EPS
LANES = 128
TILE = 16
LIFT = 50.0
FLOOR = 2.0**-41
MIB = 1024 * 1024
NOTHING = -1e30


def round_up(value, step):
    return -(-value // step) * step


def swap(value, axis, mask):
    return lax.ppermute(value, axis, [(k, k ^ mask) for k in range(lax.axis_size(axis))])


def gather_gen(gen_own):
    gens = [(gen_own, 0)]
    bit = lax.axis_size("dat") // 2
    while bit > 1:
        gens += [(swap(array, "dat", bit), mask ^ bit) for array, mask in gens]
        bit //= 2
    return [array for array, _ in gens], [mask for _, mask in gens]


def gather_column(message, column):
    span = message.shape[0]
    far = range(2, lax.axis_size("gen"), 2)
    for k, mask in enumerate(far):
        column = lax.dynamic_update_slice(column, swap(message, "gen", mask), ((k + 1) * span, 0))
    return column, [0, *far]


def pack_kernel(y_hbm_ref, g_hbm_ref, packed_ref, column_ref, own_g_ref, y_ref, g_ref, sems):
    copies = [
        pltpu.make_async_copy(y_hbm_ref, y_ref, sems.at[0]),
        pltpu.make_async_copy(g_hbm_ref, g_ref, sems.at[1]),
    ]
    for copy in copies:
        copy.start()
    for copy in copies:
        copy.wait()
    share, width = y_ref.shape
    tall = packed_ref.shape[0] - TILE
    own_g_ref[...] = g_ref[...]
    y = y_ref[...]
    wide = y.astype(jnp.float32)
    sq = jnp.sum(wide * wide, axis=1, keepdims=True)
    sq = jnp.broadcast_to(sq, (share, LANES)).T[0:1, :]
    bias = SCALE * (g_ref[...] - sq / width)
    first = bias.astype(jnp.bfloat16).astype(jnp.float32)
    rest = bias - first
    second = rest.astype(jnp.bfloat16).astype(jnp.float32)
    third = rest - second
    row = lax.broadcasted_iota(jnp.int32, (TILE, share), 0)
    pieces = jnp.where(row == 0, first, jnp.where(row == 1, second, jnp.where(row == 2, third, 0.0)))
    if share < tall:
        packed_ref[...] = jnp.zeros(packed_ref.shape, jnp.bfloat16)
    else:
        packed_ref[tall:, :] = jnp.zeros((TILE, width), jnp.bfloat16)
    packed_ref[:share, :] = y
    packed_ref[tall:, :share] = pieces.astype(jnp.bfloat16)
    column_ref[: packed_ref.shape[0], :] = packed_ref[...]


def unpack(parts, share, y_ref, b_ref):
    tall = round_up(share, TILE)
    span = tall + TILE
    batch = TILE // math.gcd(share, TILE)
    held = []
    k = 0
    for part in parts:
        for start in range(0, part.shape[0], span):
            pieces = part[start + tall : start + span, :share].astype(jnp.float32)
            bias = pieces[0:1, :] + pieces[1:2, :] + pieces[2:3, :]
            b_ref[k * share : (k + 1) * share, :] = jnp.broadcast_to(bias, (LANES, share)).T
            if batch == 1:
                y_ref[k * share : (k + 1) * share, :] = part[start : start + share, :]
            else:
                held.append(part[start : start + tall, :].astype(jnp.float32)[:share, :])
                if len(held) == batch:
                    end = (k + 1) * share
                    y_ref[end - batch * share : end, :] = jnp.concatenate(held, axis=0).astype(jnp.bfloat16)
                    held = []
            k += 1


def norm_kernel(x_ref, sq_ref, copy_ref):
    copy_ref[...] = x_ref[...]
    x = x_ref[...].astype(jnp.float32)
    square = x * x
    high = square.astype(jnp.bfloat16)
    low = (square - high.astype(jnp.float32)).astype(jnp.bfloat16)
    ones = jnp.ones((TILE, x.shape[1]), jnp.bfloat16)
    sq = jnp.zeros((TILE, x.shape[0]), jnp.float32)
    for half in (high, low):
        sq += lax.dot_general(ones, half, (((1,), (1,)), ((), ())), preferred_element_type=jnp.float32)
    for k in range(sq_ref.shape[0]):
        sq_ref[k : k + 1, :] = sq[0:1, k * LANES : (k + 1) * LANES]


def spans(total, step):
    return [(start, min(step, total - start)) for start in range(0, total, step)]


def dots(y, x):
    return lax.dot_general(y, x, (((1,), (1,)), ((), ())), preferred_element_type=jnp.float32)


def across(values, count):
    return jnp.concatenate([values] * count, axis=1)


def each_pair(xs, dots_ref, fill, visit):
    rows = xs[0].shape[0]
    half = rows // 2
    for place, x_ref in enumerate(xs):
        for k in range(2):
            fill(dots_ref.at[k], x_ref[k * half : (k + 1) * half, :])
        for k in range(2):
            visit(dots_ref.at[k], (place * rows + k * half) // LANES)


def eight(values, op):
    groups = values.reshape(values.shape[0] // 8, 8, values.shape[1])
    return op(groups, axis=0)


def fold(values, op):
    out = values[:, :LANES]
    for start in range(LANES, values.shape[1], LANES):
        out = op(out, values[:, start : start + LANES])
    return out


def row_kernel(*refs, count, share, tall, merge, unpacked):
    xs, refs = refs[:count], refs[count:]
    before, refs = refs[:merge], refs[merge:]
    if unpacked:
        y_ref, b_ref, l_ref, top_ref, e_ref, t_ref = refs
    else:
        *parts, l_ref, top_ref, e_ref, y_ref, b_ref, t_ref = refs
        unpack(parts, share, y_ref, b_ref)
    cols, width = y_ref.shape
    alpha = 2.0 * SCALE / width
    repeat = t_ref.shape[2] // LANES

    def fill(slot, x):
        slot[...] = dots(y_ref[...], x)

    def visit(slot, place):
        top = None
        for start, size in spans(cols, tall):
            here = slice(start, start + size)
            t = alpha * slot[here, :] + across(b_ref[here, :], repeat)
            slot[here, :] = t
            part = eight(t, jnp.max)
            top = part if top is None else jnp.maximum(top, part)
        base = jnp.max(top, axis=0, keepdims=True) - LIFT
        total = None
        for start, size in spans(cols, tall):
            here = slice(start, start + size)
            e = jnp.exp2(slot[here, :] - base)
            e_ref[place // repeat, here, :] = e
            part = eight(e, jnp.sum)
            total = part if total is None else total + part
        log_sum = base + jnp.log2(jnp.sum(total, axis=0, keepdims=True))
        for k in range(repeat):
            lanes = slice(k * LANES, (k + 1) * LANES)
            l_ref[place + k : place + k + 1, :] = log_sum[:, lanes]
            top_ref[place + k : place + k + 1, :] = base[:, lanes] + LIFT

    each_pair(xs, t_ref, fill, visit)
    if merge:
        l_ref[...] = merged([jnp.concatenate([log[...] for log in before], axis=0), l_ref[...]])


def merged(pieces):
    top = functools.reduce(jnp.maximum, pieces)
    return top + jnp.log2(sum(jnp.exp2(piece - top) for piece in pieces))


def column_kernel(*refs, count, share, tall, orders, masks, log_cols, segments):
    xs, refs = refs[:count], refs[count:]
    logs, refs = refs[: len(orders)], refs[len(orders) :]
    sq_ref, *data, f_ref, col_ref, l_ref, sum_ref, top_ref, t_ref = refs
    calls = sum(len(segment) for segment in segments)
    held, data = data[: 2 * calls], data[2 * calls :]
    ys, biases = data[::2], data[1::2]
    rows, width = xs[0].shape
    alpha = 2.0 * SCALE / width
    repeat = t_ref.shape[2] // LANES
    tiles = f_ref.shape[0]
    for k in range(len(orders)):
        pieces = [log[order[k] * tiles : (order[k] + 1) * tiles, :] for log, order in zip(logs, orders)]
        l_ref[k * tiles : (k + 1) * tiles, :] = merged(pieces)
    f_ref[...] = sq_ref[...] / width - (EPS * LN2) * l_ref[:tiles, :] + EPS * log_cols

    def fill(slot, x):
        offset = 0
        for y_ref in ys:
            cols = y_ref.shape[0]
            slot[offset : offset + cols, :] = dots(y_ref[...], x)
            offset += cols

    def each(visit):
        def visit_all(slot, place):
            log_here = jnp.concatenate([l_ref[place + k : place + k + 1, :] for k in range(repeat)], axis=1)
            offset = 0
            for b_ref in biases:
                for start, size in spans(b_ref.shape[0], tall):
                    here = slice(offset + start, offset + start + size)
                    bias = across(b_ref[start : start + size, :], repeat)
                    visit(here, alpha * slot[here, :] + bias - log_here)
                offset += b_ref.shape[0]

        each_pair(xs, t_ref, fill, visit_all)

    def raise_top(here, values):
        top_ref[here, :] = jnp.maximum(top_ref[here, :], fold(values, jnp.maximum))

    def add_from_top(here, values):
        sum_ref[here, :] += fold(jnp.exp2(values - across(top_ref[here, :], repeat)), jnp.add)

    offset = 0
    for segment in segments:
        pieces = []
        for first in segment:
            held_ref, e_ref, *held = held
            logs_here = l_ref[first * tiles : first * tiles + held_ref.shape[0], :]
            weights = jnp.exp2(held_ref[...] - logs_here + LIFT)
            for k in range(e_ref.shape[0]):
                scale = [weights[k * repeat + i : k * repeat + i + 1, :] for i in range(repeat)]
                pieces.append((e_ref, k, jnp.concatenate(scale, axis=1)))

        def add(index, carry, pieces=pieces, offset=offset):
            start = pl.multiple_of(index * tall, tall)
            here = pl.ds(start, tall)
            parts = [fold(e_ref[k, here, :] * scale, jnp.add) for e_ref, k, scale in pieces]
            sum_ref[pl.ds(offset + start, tall), :] = functools.reduce(jnp.add, parts)
            return carry

        lax.fori_loop(0, e_ref.shape[1] // tall, add, 0)
        offset += e_ref.shape[1]
    least = jnp.min(jnp.sum(sum_ref[...], axis=1, keepdims=True))
    top_ref[...] = jnp.full(top_ref.shape, -2.0 * LIFT, jnp.float32)

    @pl.when(jnp.logical_not(least >= FLOOR))
    def _():
        top_ref[...] = jnp.full(top_ref.shape, -jnp.inf, jnp.float32)
        each(raise_top)
        top = jnp.max(top_ref[...], axis=1, keepdims=True)
        top_ref[...] = jnp.broadcast_to(top, top_ref.shape)
        sum_ref[...] = jnp.zeros(sum_ref.shape, jnp.float32)
        each(add_from_top)

    gen, dat = lax.axis_index("gen"), lax.axis_index("dat")
    n_gen = lax.axis_size("gen")
    col_ref[...] = jnp.full(col_ref.shape, NOTHING, jnp.float32)
    for k, mask in enumerate(masks):
        here = slice(k * share, (k + 1) * share)
        total = jnp.sum(sum_ref[here, :].T, axis=0, keepdims=True)
        place = (dat ^ mask[1]) * n_gen + (gen ^ mask[0])
        col_ref[pl.ds(place, 1), :] = top_ref[here, :].T[0:1, :] + jnp.log2(total)


def per_device(gen_samples, data_samples, data_potential):
    rows, width = gen_samples.shape
    n_gen, n_dat = lax.axis_size("gen"), lax.axis_size("dat")
    share = data_samples.shape[0]
    half = share * n_gen
    cols = 2 * half
    tiles = rows // LANES
    span = round_up(share, TILE) + TILE
    own_g = data_potential.reshape(1, share)
    message, column, held_g = pl.pallas_call(
        pack_kernel,
        out_shape=(
            jax.ShapeDtypeStruct((span, width), jnp.bfloat16),
            jax.ShapeDtypeStruct((span * (n_gen // 2), width), jnp.bfloat16),
            jax.ShapeDtypeStruct((1, share), jnp.float32),
        ),
        in_specs=[pl.BlockSpec(memory_space=pltpu.HBM)] * 2,
        scratch_shapes=[
            pltpu.VMEM((share, width), jnp.bfloat16),
            pltpu.VMEM((1, share), jnp.float32),
            pltpu.SemaphoreType.DMA((2,)),
        ],
        compiler_params=pltpu.CompilerParams(vmem_limit_bytes=4 * MIB),
    )(*[pltpu.with_memory_space_constraint(array, pltpu.HBM) for array in (data_samples, own_g)])
    xs, order = gather_gen(gen_samples)
    column, far = gather_column(message, column)
    sq, xs[0] = pl.pallas_call(
        norm_kernel,
        out_shape=(
            jax.ShapeDtypeStruct((tiles, LANES), jnp.float32),
            jax.ShapeDtypeStruct((rows, width), gen_samples.dtype),
        ),
        compiler_params=pltpu.CompilerParams(vmem_limit_bytes=8 * MIB),
    )(gen_samples)
    tall = 64

    def cost(count):
        return pl.CostEstimate(
            flops=2 * rows * len(xs) * count * width,
            bytes_accessed=2 * (rows * len(xs) + count) * width,
            transcendentals=rows * len(xs) * count,
        )

    def row_pass(rows_of, parts, before=(), unpacked=None):
        count = unpacked[0].shape[0] if unpacked else len(parts) * half // 2
        logs_shape = jax.ShapeDtypeStruct((len(rows_of) * tiles, LANES), jnp.float32)
        unpacked_shapes = (
            jax.ShapeDtypeStruct((count, width), jnp.bfloat16),
            jax.ShapeDtypeStruct((count, LANES), jnp.float32),
        )
        log, top, e, *rest = pl.pallas_call(
            functools.partial(
                row_kernel,
                count=len(rows_of),
                share=share,
                tall=tall,
                merge=len(before),
                unpacked=unpacked is not None,
            ),
            out_shape=(
                logs_shape,
                logs_shape,
                jax.ShapeDtypeStruct((2 * len(rows_of), count, rows // 2), jnp.float32),
            )
            + (() if unpacked else unpacked_shapes),
            scratch_shapes=[pltpu.VMEM((2, count, rows // 2), jnp.float32)],
            compiler_params=pltpu.CompilerParams(vmem_limit_bytes=12 * MIB),
            cost_estimate=cost(count),
        )(*rows_of, *before, *(unpacked or parts))
        return log, [top, e], rest

    near = swap(column, "gen", 1)
    twin = swap(column, "dat", 1)
    log_own, held_own, data = row_pass(xs[:1], [column, twin])
    near, log_own = lax.optimization_barrier((near, log_own))
    near_twin = swap(near, "dat", 1)
    xs[1:], near = lax.optimization_barrier((xs[1:], near))
    log_others, held_others, _ = row_pass(xs[1:], [], unpacked=data)
    log, held_near, more = row_pass(xs, [near], [log_own, log_others])
    data = data + more
    near_twin, log = lax.optimization_barrier((near_twin, log))
    log, held_last, more = row_pass(xs, [near_twin], [log])
    data = data + more
    held = held_own + held_others + held_near + held_last
    segments = [[0, 1], [0], [0]]
    masks = [(g ^ a, b) for a in (0, 1) for b in (0, 1) for g in far]
    logs = [log]
    logs += [swap(logs[0], "dat", m) for m in order[1:]]
    orders = [[order.index(m ^ partner) for m in order] for partner in order]
    f, col = pl.pallas_call(
        functools.partial(
            column_kernel,
            count=len(xs),
            share=share,
            tall=tall,
            orders=orders,
            masks=masks,
            log_cols=math.log(half * n_dat),
            segments=segments,
        ),
        out_shape=(
            jax.ShapeDtypeStruct((tiles, LANES), jnp.float32),
            jax.ShapeDtypeStruct((n_dat * n_gen, share), jnp.float32),
        ),
        scratch_shapes=[
            pltpu.VMEM((len(order) * tiles, LANES), jnp.float32),
            pltpu.VMEM((cols, LANES), jnp.float32),
            pltpu.VMEM((cols, LANES), jnp.float32),
            pltpu.VMEM((2, cols, rows // 2), jnp.float32),
        ],
        compiler_params=pltpu.CompilerParams(vmem_limit_bytes=16 * MIB),
        cost_estimate=cost(cols),
    )(*xs, *logs, sq, *held, *data)
    totals = lax.all_to_all(col, ("dat", "gen"), 0, 0, tiled=True)
    top = jnp.max(totals, axis=0)
    total = top + jnp.log2(jnp.sum(jnp.exp2(totals - top[None, :]), axis=0))
    new_data = held_g[0] - (EPS * LN2) * total + EPS * math.log(rows * n_gen / half)
    return f.reshape(rows), new_data


def solution(mesh):
    in_specs = (P(("gen", "dat"), None), P(("dat", "gen"), None), P(("dat", "gen")))
    out_specs = (P(("gen", "dat")), P(("dat", "gen")))
    return jax.shard_map(per_device, mesh=mesh, in_specs=in_specs, out_specs=out_specs, check_vma=False)
```

```python
import functools
import math

import jax
import jax.numpy as jnp
from jax import lax
from jax.experimental import pallas as pl
from jax.experimental.pallas import tpu as pltpu
from jax.sharding import PartitionSpec as P

EPS = 0.05
LOG2E = 1.4426950408889634
LN2 = 0.6931471805599453
SCALE = LOG2E / EPS
LANES = 128
TILE = 16
LIFT = 50.0
FLOOR = 2.0**-41
MIB = 1024 * 1024
NOTHING = -1e30


def round_up(value, step):
    return -(-value // step) * step


def swap(value, axis, mask):
    return lax.ppermute(value, axis, [(k, k ^ mask) for k in range(lax.axis_size(axis))])


def gather_gen(gen_own):
    gens = [(gen_own, 0)]
    bit = lax.axis_size("dat") // 2
    while bit > 1:
        gens += [(swap(array, "dat", bit), mask ^ bit) for array, mask in gens]
        bit //= 2
    return [array for array, _ in gens], [mask for _, mask in gens]


def gather_column(message, column):
    masks = [0]
    bit = lax.axis_size("gen") // 2
    while bit > 1:
        held = message.shape[0]
        other = swap(message, "gen", bit)
        column = lax.dynamic_update_slice(column, other, (held, 0))
        masks += [mask ^ bit for mask in masks]
        bit //= 2
        message = column[: 2 * held] if bit > 1 else column
    return column, masks


def pack_kernel(
    y_hbm_ref, g_hbm_ref, x_hbm_ref, packed_ref, column_ref, own_g_ref, own_x_ref, y_ref, g_ref, sems
):
    copies = [
        pltpu.make_async_copy(y_hbm_ref, y_ref, sems.at[0]),
        pltpu.make_async_copy(g_hbm_ref, g_ref, sems.at[1]),
        pltpu.make_async_copy(x_hbm_ref, own_x_ref, sems.at[2]),
    ]
    for copy in copies:
        copy.start()
    for copy in copies[:2]:
        copy.wait()
    share, width = y_ref.shape
    tall = packed_ref.shape[0] - TILE
    own_g_ref[...] = g_ref[...]
    y = y_ref[...]
    wide = y.astype(jnp.float32)
    sq = jnp.sum(wide * wide, axis=1, keepdims=True)
    sq = jnp.broadcast_to(sq, (share, LANES)).T[0:1, :]
    bias = SCALE * (g_ref[...] - sq / width)
    first = bias.astype(jnp.bfloat16).astype(jnp.float32)
    rest = bias - first
    second = rest.astype(jnp.bfloat16).astype(jnp.float32)
    third = rest - second
    row = lax.broadcasted_iota(jnp.int32, (TILE, share), 0)
    pieces = jnp.where(row == 0, first, jnp.where(row == 1, second, jnp.where(row == 2, third, 0.0)))
    if share < tall:
        packed_ref[...] = jnp.zeros(packed_ref.shape, jnp.bfloat16)
    else:
        packed_ref[tall:, :] = jnp.zeros((TILE, width), jnp.bfloat16)
    packed_ref[:share, :] = y
    packed_ref[tall:, :share] = pieces.astype(jnp.bfloat16)
    column_ref[: packed_ref.shape[0], :] = packed_ref[...]
    copies[2].wait()


def unpack(parts, share, y_ref, b_ref):
    tall = round_up(share, TILE)
    span = tall + TILE
    batch = TILE // math.gcd(share, TILE)
    held = []
    k = 0
    for part in parts:
        for start in range(0, part.shape[0], span):
            pieces = part[start + tall : start + span, :share].astype(jnp.float32)
            bias = pieces[0:1, :] + pieces[1:2, :] + pieces[2:3, :]
            b_ref[k * share : (k + 1) * share, :] = jnp.broadcast_to(bias, (LANES, share)).T
            if batch == 1:
                y_ref[k * share : (k + 1) * share, :] = part[start : start + share, :]
            else:
                held.append(part[start : start + tall, :].astype(jnp.float32)[:share, :])
                if len(held) == batch:
                    end = (k + 1) * share
                    y_ref[end - batch * share : end, :] = jnp.concatenate(held, axis=0).astype(jnp.bfloat16)
                    held = []
            k += 1


def norm_kernel(x_ref, sq_ref):
    x = x_ref[...].astype(jnp.float32)
    square = x * x
    high = square.astype(jnp.bfloat16)
    low = (square - high.astype(jnp.float32)).astype(jnp.bfloat16)
    ones = jnp.ones((TILE, x.shape[1]), jnp.bfloat16)
    sq = jnp.zeros((TILE, x.shape[0]), jnp.float32)
    for half in (high, low):
        sq += lax.dot_general(ones, half, (((1,), (1,)), ((), ())), preferred_element_type=jnp.float32)
    for k in range(sq_ref.shape[0]):
        sq_ref[k : k + 1, :] = sq[0:1, k * LANES : (k + 1) * LANES]


def spans(total, step):
    return [(start, min(step, total - start)) for start in range(0, total, step)]


def dots(y, x):
    return lax.dot_general(y, x, (((1,), (1,)), ((), ())), preferred_element_type=jnp.float32)


def across(values, count):
    return jnp.concatenate([values] * count, axis=1)


def each_pair(xs, dots_ref, fill, visit):
    rows = xs[0].shape[0]
    half = rows // 2
    for place, x_ref in enumerate(xs):
        for k in range(2):
            fill(dots_ref.at[k], x_ref[k * half : (k + 1) * half, :])
        for k in range(2):
            visit(dots_ref.at[k], (place * rows + k * half) // LANES)


def eight(values, op):
    groups = values.reshape(values.shape[0] // 8, 8, values.shape[1])
    return op(groups, axis=0)


def fold(values, op):
    out = values[:, :LANES]
    for start in range(LANES, values.shape[1], LANES):
        out = op(out, values[:, start : start + LANES])
    return out


def row_kernel(*refs, count, share, tall, merge, unpacked):
    xs, refs = refs[:count], refs[count:]
    before, refs = refs[:merge], refs[merge:]
    if unpacked:
        y_ref, b_ref, l_ref, top_ref, e_ref, t_ref = refs
    else:
        *parts, l_ref, top_ref, e_ref, y_ref, b_ref, t_ref = refs
        unpack(parts, share, y_ref, b_ref)
    cols, width = y_ref.shape
    alpha = 2.0 * SCALE / width
    repeat = t_ref.shape[2] // LANES

    def fill(slot, x):
        slot[...] = dots(y_ref[...], x)

    def visit(slot, place):
        top = None
        for start, size in spans(cols, tall):
            here = slice(start, start + size)
            t = alpha * slot[here, :] + across(b_ref[here, :], repeat)
            slot[here, :] = t
            part = eight(t, jnp.max)
            top = part if top is None else jnp.maximum(top, part)
        base = jnp.max(top, axis=0, keepdims=True) - LIFT
        total = None
        for start, size in spans(cols, tall):
            here = slice(start, start + size)
            e = jnp.exp2(slot[here, :] - base)
            e_ref[place // repeat, here, :] = e
            part = eight(e, jnp.sum)
            total = part if total is None else total + part
        log_sum = base + jnp.log2(jnp.sum(total, axis=0, keepdims=True))
        for k in range(repeat):
            lanes = slice(k * LANES, (k + 1) * LANES)
            l_ref[place + k : place + k + 1, :] = log_sum[:, lanes]
            top_ref[place + k : place + k + 1, :] = base[:, lanes] + LIFT

    each_pair(xs, t_ref, fill, visit)
    if merge:
        l_ref[...] = merged([jnp.concatenate([log[...] for log in before], axis=0), l_ref[...]])


def merged(pieces):
    top = functools.reduce(jnp.maximum, pieces)
    return top + jnp.log2(sum(jnp.exp2(piece - top) for piece in pieces))


def column_kernel(*refs, count, share, tall, orders, masks, log_cols, segments):
    xs, refs = refs[:count], refs[count:]
    logs, refs = refs[: len(orders)], refs[len(orders) :]
    sq_ref, *data, f_ref, col_ref, l_ref, sum_ref, top_ref, t_ref = refs
    calls = sum(len(segment) for segment in segments)
    held, data = data[: 2 * calls], data[2 * calls :]
    ys, biases = data[::2], data[1::2]
    rows, width = xs[0].shape
    alpha = 2.0 * SCALE / width
    repeat = t_ref.shape[2] // LANES
    tiles = f_ref.shape[0]
    for k in range(len(orders)):
        pieces = [log[order[k] * tiles : (order[k] + 1) * tiles, :] for log, order in zip(logs, orders)]
        l_ref[k * tiles : (k + 1) * tiles, :] = merged(pieces)
    f_ref[...] = sq_ref[...] / width - (EPS * LN2) * l_ref[:tiles, :] + EPS * log_cols

    def fill(slot, x):
        offset = 0
        for y_ref in ys:
            cols = y_ref.shape[0]
            slot[offset : offset + cols, :] = dots(y_ref[...], x)
            offset += cols

    def each(visit):
        def visit_all(slot, place):
            log_here = jnp.concatenate([l_ref[place + k : place + k + 1, :] for k in range(repeat)], axis=1)
            offset = 0
            for b_ref in biases:
                for start, size in spans(b_ref.shape[0], tall):
                    here = slice(offset + start, offset + start + size)
                    bias = across(b_ref[start : start + size, :], repeat)
                    visit(here, alpha * slot[here, :] + bias - log_here)
                offset += b_ref.shape[0]

        each_pair(xs, t_ref, fill, visit_all)

    def raise_top(here, values):
        top_ref[here, :] = jnp.maximum(top_ref[here, :], fold(values, jnp.maximum))

    def add_from_top(here, values):
        sum_ref[here, :] += fold(jnp.exp2(values - across(top_ref[here, :], repeat)), jnp.add)

    offset = 0
    for segment in segments:
        pieces = []
        for first in segment:
            held_ref, e_ref, *held = held
            logs_here = l_ref[first * tiles : first * tiles + held_ref.shape[0], :]
            weights = jnp.exp2(held_ref[...] - logs_here + LIFT)
            for k in range(e_ref.shape[0]):
                scale = [weights[k * repeat + i : k * repeat + i + 1, :] for i in range(repeat)]
                pieces.append((e_ref, k, jnp.concatenate(scale, axis=1)))

        def add(index, carry, pieces=pieces, offset=offset):
            start = pl.multiple_of(index * tall, tall)
            here = pl.ds(start, tall)
            parts = [fold(e_ref[k, here, :] * scale, jnp.add) for e_ref, k, scale in pieces]
            sum_ref[pl.ds(offset + start, tall), :] = functools.reduce(jnp.add, parts)
            return carry

        lax.fori_loop(0, e_ref.shape[1] // tall, add, 0)
        offset += e_ref.shape[1]
    least = jnp.min(jnp.sum(sum_ref[...], axis=1, keepdims=True))
    top_ref[...] = jnp.full(top_ref.shape, -2.0 * LIFT, jnp.float32)

    @pl.when(jnp.logical_not(least >= FLOOR))
    def _():
        top_ref[...] = jnp.full(top_ref.shape, -jnp.inf, jnp.float32)
        each(raise_top)
        top = jnp.max(top_ref[...], axis=1, keepdims=True)
        top_ref[...] = jnp.broadcast_to(top, top_ref.shape)
        sum_ref[...] = jnp.zeros(sum_ref.shape, jnp.float32)
        each(add_from_top)

    gen, dat = lax.axis_index("gen"), lax.axis_index("dat")
    n_gen = lax.axis_size("gen")
    col_ref[...] = jnp.full(col_ref.shape, NOTHING, jnp.float32)
    for k, mask in enumerate(masks):
        here = slice(k * share, (k + 1) * share)
        total = jnp.sum(sum_ref[here, :].T, axis=0, keepdims=True)
        place = (dat ^ mask[1]) * n_gen + (gen ^ mask[0])
        col_ref[pl.ds(place, 1), :] = top_ref[here, :].T[0:1, :] + jnp.log2(total)


def per_device(gen_samples, data_samples, data_potential):
    rows, width = gen_samples.shape
    n_gen, n_dat = lax.axis_size("gen"), lax.axis_size("dat")
    share = data_samples.shape[0]
    half = share * n_gen
    cols = 2 * half
    tiles = rows // LANES
    span = round_up(share, TILE) + TILE
    own_g = data_potential.reshape(1, share)
    message, column, held_g, held_x = pl.pallas_call(
        pack_kernel,
        out_shape=(
            jax.ShapeDtypeStruct((span, width), jnp.bfloat16),
            jax.ShapeDtypeStruct((span * (n_gen // 2), width), jnp.bfloat16),
            jax.ShapeDtypeStruct((1, share), jnp.float32),
            jax.ShapeDtypeStruct((rows, width), gen_samples.dtype),
        ),
        in_specs=[pl.BlockSpec(memory_space=pltpu.HBM)] * 3,
        scratch_shapes=[
            pltpu.VMEM((share, width), jnp.bfloat16),
            pltpu.VMEM((1, share), jnp.float32),
            pltpu.SemaphoreType.DMA((3,)),
        ],
        compiler_params=pltpu.CompilerParams(vmem_limit_bytes=4 * MIB),
    )(*[pltpu.with_memory_space_constraint(array, pltpu.HBM) for array in (data_samples, own_g, gen_samples)])
    xs, order = gather_gen(gen_samples)
    column, far = gather_column(message, column)
    xs[1:], xs[0] = lax.optimization_barrier((xs[1:], held_x))
    sq = pl.pallas_call(
        norm_kernel,
        out_shape=jax.ShapeDtypeStruct((tiles, LANES), jnp.float32),
        compiler_params=pltpu.CompilerParams(vmem_limit_bytes=8 * MIB),
        cost_estimate=pl.CostEstimate(flops=8 * rows * width * width, bytes_accessed=16 * MIB, transcendentals=0),
    )(xs[0])
    tall = 64

    def cost(count):
        return pl.CostEstimate(
            flops=2 * rows * len(xs) * count * width,
            bytes_accessed=2 * (rows * len(xs) + count) * width,
            transcendentals=rows * len(xs) * count,
        )

    def row_pass(rows_of, parts, before=(), unpacked=None):
        count = unpacked[0].shape[0] if unpacked else len(parts) * half // 2
        logs_shape = jax.ShapeDtypeStruct((len(rows_of) * tiles, LANES), jnp.float32)
        unpacked_shapes = (
            jax.ShapeDtypeStruct((count, width), jnp.bfloat16),
            jax.ShapeDtypeStruct((count, LANES), jnp.float32),
        )
        log, top, e, *rest = pl.pallas_call(
            functools.partial(
                row_kernel,
                count=len(rows_of),
                share=share,
                tall=tall,
                merge=len(before),
                unpacked=unpacked is not None,
            ),
            out_shape=(
                logs_shape,
                logs_shape,
                jax.ShapeDtypeStruct((2 * len(rows_of), count, rows // 2), jnp.float32),
            )
            + (() if unpacked else unpacked_shapes),
            scratch_shapes=[pltpu.VMEM((2, count, rows // 2), jnp.float32)],
            compiler_params=pltpu.CompilerParams(vmem_limit_bytes=12 * MIB),
            cost_estimate=cost(count),
        )(*rows_of, *before, *(unpacked or parts))
        return log, [top, e], rest

    near = swap(column, "gen", 1)
    twin = swap(column, "dat", 1)
    log_own, held_own, data = row_pass(xs[:1], [column, twin])
    near_twin = swap(near, "dat", 1)
    log_others, held_others, _ = row_pass(xs[1:], [], unpacked=data)
    log, held_near, more = row_pass(xs, [near], [log_own, log_others])
    data = data + more
    near_twin, log = lax.optimization_barrier((near_twin, log))
    log, held_last, more = row_pass(xs, [near_twin], [log])
    data = data + more
    held = held_own + held_others + held_near + held_last
    segments = [[0, 1], [0], [0]]
    masks = [(g ^ a, b) for a in (0, 1) for b in (0, 1) for g in far]
    logs = [log]
    logs += [swap(logs[0], "dat", m) for m in order[1:]]
    orders = [[order.index(m ^ partner) for m in order] for partner in order]
    f, col = pl.pallas_call(
        functools.partial(
            column_kernel,
            count=len(xs),
            share=share,
            tall=tall,
            orders=orders,
            masks=masks,
            log_cols=math.log(half * n_dat),
            segments=segments,
        ),
        out_shape=(
            jax.ShapeDtypeStruct((tiles, LANES), jnp.float32),
            jax.ShapeDtypeStruct((n_dat * n_gen, share), jnp.float32),
        ),
        scratch_shapes=[
            pltpu.VMEM((len(order) * tiles, LANES), jnp.float32),
            pltpu.VMEM((cols, LANES), jnp.float32),
            pltpu.VMEM((cols, LANES), jnp.float32),
            pltpu.VMEM((2, cols, rows // 2), jnp.float32),
        ],
        compiler_params=pltpu.CompilerParams(vmem_limit_bytes=16 * MIB),
        cost_estimate=cost(cols),
    )(*xs, *logs, sq, *held, *data)
    totals = lax.all_to_all(col, ("dat", "gen"), 0, 0, tiled=True)
    top = jnp.max(totals, axis=0)
    total = top + jnp.log2(jnp.sum(jnp.exp2(totals - top[None, :]), axis=0))
    new_data = held_g[0] - (EPS * LN2) * total + EPS * math.log(rows * n_gen / half)
    return f.reshape(rows), new_data


def solution(mesh):
    in_specs = (P(("gen", "dat"), None), P(("dat", "gen"), None), P(("dat", "gen")))
    out_specs = (P(("gen", "dat")), P(("dat", "gen")))
    return jax.shard_map(per_device, mesh=mesh, in_specs=in_specs, out_specs=out_specs, check_vma=False)
```

```python
import functools
import math

import jax
import jax.numpy as jnp
from jax import lax
from jax.experimental import pallas as pl
from jax.experimental.pallas import tpu as pltpu
from jax.sharding import PartitionSpec as P

EPS = 0.05
LOG2E = 1.4426950408889634
LN2 = 0.6931471805599453
SCALE = LOG2E / EPS
LANES = 128
TILE = 16
LIFT = 50.0
FLOOR = 2.0**-41
MIB = 1024 * 1024
NOTHING = -1e30


def round_up(value, step):
    return -(-value // step) * step


def swap(value, axis, mask):
    return lax.ppermute(value, axis, [(k, k ^ mask) for k in range(lax.axis_size(axis))])


def gather_gen(gen_own):
    gens = [(gen_own, 0)]
    bit = lax.axis_size("dat") // 2
    while bit > 1:
        gens += [(swap(array, "dat", bit), mask ^ bit) for array, mask in gens]
        bit //= 2
    return [array for array, _ in gens], [mask for _, mask in gens]


def gather_column(message, column):
    span = message.shape[0]
    far = range(2, lax.axis_size("gen"), 2)
    for k, mask in enumerate(far):
        column = lax.dynamic_update_slice(column, swap(message, "gen", mask), ((k + 1) * span, 0))
    return column, [0, *far]


def pack_kernel(
    y_hbm_ref, g_hbm_ref, x_hbm_ref, packed_ref, column_ref, own_g_ref, own_x_ref, y_ref, g_ref, sems
):
    copies = [
        pltpu.make_async_copy(y_hbm_ref, y_ref, sems.at[0]),
        pltpu.make_async_copy(g_hbm_ref, g_ref, sems.at[1]),
        pltpu.make_async_copy(x_hbm_ref, own_x_ref, sems.at[2]),
    ]
    for copy in copies:
        copy.start()
    for copy in copies[:2]:
        copy.wait()
    share, width = y_ref.shape
    tall = packed_ref.shape[0] - TILE
    own_g_ref[...] = g_ref[...]
    y = y_ref[...]
    wide = y.astype(jnp.float32)
    sq = jnp.sum(wide * wide, axis=1, keepdims=True)
    sq = jnp.broadcast_to(sq, (share, LANES)).T[0:1, :]
    bias = SCALE * (g_ref[...] - sq / width)
    first = bias.astype(jnp.bfloat16).astype(jnp.float32)
    rest = bias - first
    second = rest.astype(jnp.bfloat16).astype(jnp.float32)
    third = rest - second
    row = lax.broadcasted_iota(jnp.int32, (TILE, share), 0)
    pieces = jnp.where(row == 0, first, jnp.where(row == 1, second, jnp.where(row == 2, third, 0.0)))
    if share < tall:
        packed_ref[...] = jnp.zeros(packed_ref.shape, jnp.bfloat16)
    else:
        packed_ref[tall:, :] = jnp.zeros((TILE, width), jnp.bfloat16)
    packed_ref[:share, :] = y
    packed_ref[tall:, :share] = pieces.astype(jnp.bfloat16)
    column_ref[: packed_ref.shape[0], :] = packed_ref[...]
    copies[2].wait()


def unpack(parts, share, y_ref, b_ref):
    tall = round_up(share, TILE)
    span = tall + TILE
    batch = TILE // math.gcd(share, TILE)
    held = []
    k = 0
    for part in parts:
        for start in range(0, part.shape[0], span):
            pieces = part[start + tall : start + span, :share].astype(jnp.float32)
            bias = pieces[0:1, :] + pieces[1:2, :] + pieces[2:3, :]
            b_ref[k * share : (k + 1) * share, :] = jnp.broadcast_to(bias, (LANES, share)).T
            if batch == 1:
                y_ref[k * share : (k + 1) * share, :] = part[start : start + share, :]
            else:
                held.append(part[start : start + tall, :].astype(jnp.float32)[:share, :])
                if len(held) == batch:
                    end = (k + 1) * share
                    y_ref[end - batch * share : end, :] = jnp.concatenate(held, axis=0).astype(jnp.bfloat16)
                    held = []
            k += 1


def norm_kernel(x_ref, sq_ref):
    x = x_ref[...].astype(jnp.float32)
    square = x * x
    high = square.astype(jnp.bfloat16)
    low = (square - high.astype(jnp.float32)).astype(jnp.bfloat16)
    ones = jnp.ones((TILE, x.shape[1]), jnp.bfloat16)
    sq = jnp.zeros((TILE, x.shape[0]), jnp.float32)
    for half in (high, low):
        sq += lax.dot_general(ones, half, (((1,), (1,)), ((), ())), preferred_element_type=jnp.float32)
    for k in range(sq_ref.shape[0]):
        sq_ref[k : k + 1, :] = sq[0:1, k * LANES : (k + 1) * LANES]


def spans(total, step):
    return [(start, min(step, total - start)) for start in range(0, total, step)]


def dots(y, x):
    return lax.dot_general(y, x, (((1,), (1,)), ((), ())), preferred_element_type=jnp.float32)


def across(values, count):
    return jnp.concatenate([values] * count, axis=1)


def each_pair(xs, dots_ref, fill, visit):
    rows = xs[0].shape[0]
    half = rows // 2
    for place, x_ref in enumerate(xs):
        for k in range(2):
            fill(dots_ref.at[k], x_ref[k * half : (k + 1) * half, :])
        for k in range(2):
            visit(dots_ref.at[k], (place * rows + k * half) // LANES)


def eight(values, op):
    groups = values.reshape(values.shape[0] // 8, 8, values.shape[1])
    return op(groups, axis=0)


def fold(values, op):
    out = values[:, :LANES]
    for start in range(LANES, values.shape[1], LANES):
        out = op(out, values[:, start : start + LANES])
    return out


def row_kernel(*refs, count, share, tall, merge, unpacked):
    xs, refs = refs[:count], refs[count:]
    before, refs = refs[:merge], refs[merge:]
    if unpacked:
        y_ref, b_ref, l_ref, top_ref, e_ref, t_ref = refs
    else:
        *parts, l_ref, top_ref, e_ref, y_ref, b_ref, t_ref = refs
        unpack(parts, share, y_ref, b_ref)
    cols, width = y_ref.shape
    alpha = 2.0 * SCALE / width
    repeat = t_ref.shape[2] // LANES

    def fill(slot, x):
        slot[...] = dots(y_ref[...], x)

    def visit(slot, place):
        top = None
        for start, size in spans(cols, tall):
            here = slice(start, start + size)
            t = alpha * slot[here, :] + across(b_ref[here, :], repeat)
            slot[here, :] = t
            part = eight(t, jnp.max)
            top = part if top is None else jnp.maximum(top, part)
        base = jnp.max(top, axis=0, keepdims=True) - LIFT
        total = None
        for start, size in spans(cols, tall):
            here = slice(start, start + size)
            e = jnp.exp2(slot[here, :] - base)
            e_ref[place // repeat, here, :] = e
            part = eight(e, jnp.sum)
            total = part if total is None else total + part
        log_sum = base + jnp.log2(jnp.sum(total, axis=0, keepdims=True))
        for k in range(repeat):
            lanes = slice(k * LANES, (k + 1) * LANES)
            l_ref[place + k : place + k + 1, :] = log_sum[:, lanes]
            top_ref[place + k : place + k + 1, :] = base[:, lanes] + LIFT

    each_pair(xs, t_ref, fill, visit)
    if merge:
        l_ref[...] = merged([jnp.concatenate([log[...] for log in before], axis=0), l_ref[...]])


def merged(pieces):
    top = functools.reduce(jnp.maximum, pieces)
    return top + jnp.log2(sum(jnp.exp2(piece - top) for piece in pieces))


def column_kernel(*refs, count, share, tall, orders, masks, log_cols, segments):
    xs, refs = refs[:count], refs[count:]
    logs, refs = refs[: len(orders)], refs[len(orders) :]
    sq_ref, *data, f_ref, col_ref, l_ref, sum_ref, top_ref, t_ref = refs
    calls = sum(len(segment) for segment in segments)
    held, data = data[: 2 * calls], data[2 * calls :]
    ys, biases = data[::2], data[1::2]
    rows, width = xs[0].shape
    alpha = 2.0 * SCALE / width
    repeat = t_ref.shape[2] // LANES
    tiles = f_ref.shape[0]
    for k in range(len(orders)):
        pieces = [log[order[k] * tiles : (order[k] + 1) * tiles, :] for log, order in zip(logs, orders)]
        l_ref[k * tiles : (k + 1) * tiles, :] = merged(pieces)
    f_ref[...] = sq_ref[...] / width - (EPS * LN2) * l_ref[:tiles, :] + EPS * log_cols

    def fill(slot, x):
        offset = 0
        for y_ref in ys:
            cols = y_ref.shape[0]
            slot[offset : offset + cols, :] = dots(y_ref[...], x)
            offset += cols

    def each(visit):
        def visit_all(slot, place):
            log_here = jnp.concatenate([l_ref[place + k : place + k + 1, :] for k in range(repeat)], axis=1)
            offset = 0
            for b_ref in biases:
                for start, size in spans(b_ref.shape[0], tall):
                    here = slice(offset + start, offset + start + size)
                    bias = across(b_ref[start : start + size, :], repeat)
                    visit(here, alpha * slot[here, :] + bias - log_here)
                offset += b_ref.shape[0]

        each_pair(xs, t_ref, fill, visit_all)

    def raise_top(here, values):
        top_ref[here, :] = jnp.maximum(top_ref[here, :], fold(values, jnp.maximum))

    def add_from_top(here, values):
        sum_ref[here, :] += fold(jnp.exp2(values - across(top_ref[here, :], repeat)), jnp.add)

    offset = 0
    for segment in segments:
        pieces = []
        for first in segment:
            held_ref, e_ref, *held = held
            logs_here = l_ref[first * tiles : first * tiles + held_ref.shape[0], :]
            weights = jnp.exp2(held_ref[...] - logs_here + LIFT)
            for k in range(e_ref.shape[0]):
                scale = [weights[k * repeat + i : k * repeat + i + 1, :] for i in range(repeat)]
                pieces.append((e_ref, k, jnp.concatenate(scale, axis=1)))

        def add(index, carry, pieces=pieces, offset=offset):
            start = pl.multiple_of(index * tall, tall)
            here = pl.ds(start, tall)
            parts = [fold(e_ref[k, here, :] * scale, jnp.add) for e_ref, k, scale in pieces]
            sum_ref[pl.ds(offset + start, tall), :] = functools.reduce(jnp.add, parts)
            return carry

        lax.fori_loop(0, e_ref.shape[1] // tall, add, 0)
        offset += e_ref.shape[1]
    least = jnp.min(jnp.sum(sum_ref[...], axis=1, keepdims=True))
    top_ref[...] = jnp.full(top_ref.shape, -2.0 * LIFT, jnp.float32)

    @pl.when(jnp.logical_not(least >= FLOOR))
    def _():
        top_ref[...] = jnp.full(top_ref.shape, -jnp.inf, jnp.float32)
        each(raise_top)
        top = jnp.max(top_ref[...], axis=1, keepdims=True)
        top_ref[...] = jnp.broadcast_to(top, top_ref.shape)
        sum_ref[...] = jnp.zeros(sum_ref.shape, jnp.float32)
        each(add_from_top)

    gen, dat = lax.axis_index("gen"), lax.axis_index("dat")
    n_gen = lax.axis_size("gen")
    col_ref[...] = jnp.full(col_ref.shape, NOTHING, jnp.float32)
    for k, mask in enumerate(masks):
        here = slice(k * share, (k + 1) * share)
        total = jnp.sum(sum_ref[here, :].T, axis=0, keepdims=True)
        place = (dat ^ mask[1]) * n_gen + (gen ^ mask[0])
        col_ref[pl.ds(place, 1), :] = top_ref[here, :].T[0:1, :] + jnp.log2(total)


def per_device(gen_samples, data_samples, data_potential):
    rows, width = gen_samples.shape
    n_gen, n_dat = lax.axis_size("gen"), lax.axis_size("dat")
    share = data_samples.shape[0]
    half = share * n_gen
    cols = 2 * half
    tiles = rows // LANES
    span = round_up(share, TILE) + TILE
    own_g = data_potential.reshape(1, share)
    message, column, held_g, held_x = pl.pallas_call(
        pack_kernel,
        out_shape=(
            jax.ShapeDtypeStruct((span, width), jnp.bfloat16),
            jax.ShapeDtypeStruct((span * (n_gen // 2), width), jnp.bfloat16),
            jax.ShapeDtypeStruct((1, share), jnp.float32),
            jax.ShapeDtypeStruct((rows, width), gen_samples.dtype),
        ),
        in_specs=[pl.BlockSpec(memory_space=pltpu.HBM)] * 3,
        scratch_shapes=[
            pltpu.VMEM((share, width), jnp.bfloat16),
            pltpu.VMEM((1, share), jnp.float32),
            pltpu.SemaphoreType.DMA((3,)),
        ],
        compiler_params=pltpu.CompilerParams(vmem_limit_bytes=4 * MIB),
    )(*[pltpu.with_memory_space_constraint(array, pltpu.HBM) for array in (data_samples, own_g, gen_samples)])
    xs, order = gather_gen(gen_samples)
    column, far = gather_column(message, column)
    xs[0] = held_x
    xs[1:], norm_x = lax.optimization_barrier((xs[1:], held_x))
    sq = pl.pallas_call(
        norm_kernel,
        out_shape=jax.ShapeDtypeStruct((tiles, LANES), jnp.float32),
        compiler_params=pltpu.CompilerParams(vmem_limit_bytes=8 * MIB),
        cost_estimate=pl.CostEstimate(flops=8 * rows * width * width, bytes_accessed=4 * MIB, transcendentals=0),
    )(norm_x)
    xs[1:], sq = lax.optimization_barrier((xs[1:], sq))
    tall = 64

    def cost(count):
        return pl.CostEstimate(
            flops=2 * rows * len(xs) * count * width,
            bytes_accessed=2 * (rows * len(xs) + count) * width,
            transcendentals=rows * len(xs) * count,
        )

    def row_pass(rows_of, parts, before=(), unpacked=None):
        count = unpacked[0].shape[0] if unpacked else len(parts) * half // 2
        logs_shape = jax.ShapeDtypeStruct((len(rows_of) * tiles, LANES), jnp.float32)
        unpacked_shapes = (
            jax.ShapeDtypeStruct((count, width), jnp.bfloat16),
            jax.ShapeDtypeStruct((count, LANES), jnp.float32),
        )
        log, top, e, *rest = pl.pallas_call(
            functools.partial(
                row_kernel,
                count=len(rows_of),
                share=share,
                tall=tall,
                merge=len(before),
                unpacked=unpacked is not None,
            ),
            out_shape=(
                logs_shape,
                logs_shape,
                jax.ShapeDtypeStruct((2 * len(rows_of), count, rows // 2), jnp.float32),
            )
            + (() if unpacked else unpacked_shapes),
            scratch_shapes=[pltpu.VMEM((2, count, rows // 2), jnp.float32)],
            compiler_params=pltpu.CompilerParams(vmem_limit_bytes=12 * MIB),
            cost_estimate=cost(count),
        )(*rows_of, *before, *(unpacked or parts))
        return log, [top, e], rest

    near = swap(column, "gen", 1)
    twin = swap(column, "dat", 1)
    log_own, held_own, data = row_pass(xs[:1], [column])
    near, log_own = lax.optimization_barrier((near, log_own))
    near_twin = swap(near, "dat", 1)
    twin, near = lax.optimization_barrier((twin, near))
    log_others, held_others, _ = row_pass(xs[1:], [], unpacked=data)
    log, held_both, more = row_pass(xs, [near, twin], [log_own, log_others])
    data = data + more
    near_twin, log = lax.optimization_barrier((near_twin, log))
    log, held_last, more = row_pass(xs, [near_twin], [log])
    data = data + more
    held = held_own + held_others + held_both + held_last
    segments = [[0, 1], [0], [0]]
    masks = [(g ^ a, b) for a, b in ((0, 0), (1, 0), (0, 1), (1, 1)) for g in far]
    logs = [log]
    logs += [swap(logs[0], "dat", m) for m in order[1:]]
    orders = [[order.index(m ^ partner) for m in order] for partner in order]
    f, col = pl.pallas_call(
        functools.partial(
            column_kernel,
            count=len(xs),
            share=share,
            tall=tall,
            orders=orders,
            masks=masks,
            log_cols=math.log(half * n_dat),
            segments=segments,
        ),
        out_shape=(
            jax.ShapeDtypeStruct((tiles, LANES), jnp.float32),
            jax.ShapeDtypeStruct((n_dat * n_gen, share), jnp.float32),
        ),
        scratch_shapes=[
            pltpu.VMEM((len(order) * tiles, LANES), jnp.float32),
            pltpu.VMEM((cols, LANES), jnp.float32),
            pltpu.VMEM((cols, LANES), jnp.float32),
            pltpu.VMEM((2, cols, rows // 2), jnp.float32),
        ],
        compiler_params=pltpu.CompilerParams(vmem_limit_bytes=16 * MIB),
        cost_estimate=cost(cols),
    )(*xs, *logs, sq, *held, *data)
    totals = lax.all_to_all(col, ("dat", "gen"), 0, 0, tiled=True)
    top = jnp.max(totals, axis=0)
    total = top + jnp.log2(jnp.sum(jnp.exp2(totals - top[None, :]), axis=0))
    new_data = held_g[0] - (EPS * LN2) * total + EPS * math.log(rows * n_gen / half)
    return f.reshape(rows), new_data


def solution(mesh):
    in_specs = (P(("gen", "dat"), None), P(("dat", "gen"), None), P(("dat", "gen")))
    out_specs = (P(("gen", "dat")), P(("dat", "gen")))
    return jax.shard_map(per_device, mesh=mesh, in_specs=in_specs, out_specs=out_specs, check_vma=False)
```

```python
import functools
import math

import jax
import jax.numpy as jnp
from jax import lax
from jax.experimental import pallas as pl
from jax.experimental.pallas import tpu as pltpu
from jax.sharding import PartitionSpec as P

EPS = 0.05
LOG2E = 1.4426950408889634
LN2 = 0.6931471805599453
SCALE = LOG2E / EPS
LANES = 128
TILE = 16
LIFT = 50.0
FLOOR = 2.0**-41
MIB = 1024 * 1024
NOTHING = -1e30


def round_up(value, step):
    return -(-value // step) * step


def swap(value, axis, mask):
    return lax.ppermute(value, axis, [(k, k ^ mask) for k in range(lax.axis_size(axis))])


def gather_gen(gen_own):
    gens = [(gen_own, 0)]
    bit = lax.axis_size("dat") // 2
    while bit > 1:
        gens += [(swap(array, "dat", bit), mask ^ bit) for array, mask in gens]
        bit //= 2
    return [array for array, _ in gens], [mask for _, mask in gens]


def gather_column(message, column):
    span = message.shape[0]
    far = range(2, lax.axis_size("gen"), 2)
    for k, mask in enumerate(far):
        column = lax.dynamic_update_slice(column, swap(message, "gen", mask), ((k + 1) * span, 0))
    return column, [0, *far]


def pack_kernel(
    y_hbm_ref, g_hbm_ref, x_hbm_ref, packed_ref, column_ref, own_g_ref, own_x_ref, y_ref, g_ref, sems
):
    copies = [
        pltpu.make_async_copy(y_hbm_ref, y_ref, sems.at[0]),
        pltpu.make_async_copy(g_hbm_ref, g_ref, sems.at[1]),
        pltpu.make_async_copy(x_hbm_ref, own_x_ref, sems.at[2]),
    ]
    for copy in copies:
        copy.start()
    for copy in copies[:2]:
        copy.wait()
    share, width = y_ref.shape
    tall = packed_ref.shape[0] - TILE
    own_g_ref[...] = g_ref[...]
    y = y_ref[...]
    wide = y.astype(jnp.float32)
    sq = jnp.sum(wide * wide, axis=1, keepdims=True)
    sq = jnp.broadcast_to(sq, (share, LANES)).T[0:1, :]
    bias = SCALE * (g_ref[...] - sq / width)
    first = bias.astype(jnp.bfloat16).astype(jnp.float32)
    rest = bias - first
    second = rest.astype(jnp.bfloat16).astype(jnp.float32)
    third = rest - second
    row = lax.broadcasted_iota(jnp.int32, (TILE, share), 0)
    pieces = jnp.where(row == 0, first, jnp.where(row == 1, second, jnp.where(row == 2, third, 0.0)))
    if share < tall:
        packed_ref[...] = jnp.zeros(packed_ref.shape, jnp.bfloat16)
    else:
        packed_ref[tall:, :] = jnp.zeros((TILE, width), jnp.bfloat16)
    packed_ref[:share, :] = y
    packed_ref[tall:, :share] = pieces.astype(jnp.bfloat16)
    column_ref[: packed_ref.shape[0], :] = packed_ref[...]
    copies[2].wait()


def unpack(parts, share, y_ref, b_ref):
    tall = round_up(share, TILE)
    span = tall + TILE
    batch = TILE // math.gcd(share, TILE)
    held = []
    k = 0
    for part in parts:
        for start in range(0, part.shape[0], span):
            pieces = part[start + tall : start + span, :share].astype(jnp.float32)
            bias = pieces[0:1, :] + pieces[1:2, :] + pieces[2:3, :]
            b_ref[k * share : (k + 1) * share, :] = jnp.broadcast_to(bias, (LANES, share)).T
            if batch == 1:
                y_ref[k * share : (k + 1) * share, :] = part[start : start + share, :]
            else:
                held.append(part[start : start + tall, :].astype(jnp.float32)[:share, :])
                if len(held) == batch:
                    end = (k + 1) * share
                    y_ref[end - batch * share : end, :] = jnp.concatenate(held, axis=0).astype(jnp.bfloat16)
                    held = []
            k += 1


def norm_kernel(x_ref, sq_ref):
    x = x_ref[...].astype(jnp.float32)
    square = x * x
    high = square.astype(jnp.bfloat16)
    low = (square - high.astype(jnp.float32)).astype(jnp.bfloat16)
    ones = jnp.ones((TILE, x.shape[1]), jnp.bfloat16)
    sq = jnp.zeros((TILE, x.shape[0]), jnp.float32)
    for half in (high, low):
        sq += lax.dot_general(ones, half, (((1,), (1,)), ((), ())), preferred_element_type=jnp.float32)
    for k in range(sq_ref.shape[0]):
        sq_ref[k : k + 1, :] = sq[0:1, k * LANES : (k + 1) * LANES]


def spans(total, step):
    return [(start, min(step, total - start)) for start in range(0, total, step)]


def dots(y, x):
    return lax.dot_general(y, x, (((1,), (1,)), ((), ())), preferred_element_type=jnp.float32)


def across(values, count):
    return jnp.concatenate([values] * count, axis=1)


def each_pair(xs, dots_ref, fill, visit):
    rows = xs[0].shape[0]
    half = rows // 2
    for place, x_ref in enumerate(xs):
        for k in range(2):
            fill(dots_ref.at[k], x_ref[k * half : (k + 1) * half, :])
        for k in range(2):
            visit(dots_ref.at[k], (place * rows + k * half) // LANES)


def eight(values, op):
    groups = values.reshape(values.shape[0] // 8, 8, values.shape[1])
    return op(groups, axis=0)


def fold(values, op):
    out = values[:, :LANES]
    for start in range(LANES, values.shape[1], LANES):
        out = op(out, values[:, start : start + LANES])
    return out


def row_kernel(*refs, count, share, tall, merge, unpacked):
    xs, refs = refs[:count], refs[count:]
    before, refs = refs[:merge], refs[merge:]
    if unpacked:
        y_ref, b_ref, l_ref, top_ref, e_ref, t_ref = refs
    else:
        *parts, l_ref, top_ref, e_ref, y_ref, b_ref, t_ref = refs
        unpack(parts, share, y_ref, b_ref)
    cols, width = y_ref.shape
    alpha = 2.0 * SCALE / width
    repeat = t_ref.shape[2] // LANES

    def fill(slot, x):
        slot[...] = dots(y_ref[...], x)

    def visit(slot, place):
        top = None
        for start, size in spans(cols, tall):
            here = slice(start, start + size)
            t = alpha * slot[here, :] + across(b_ref[here, :], repeat)
            slot[here, :] = t
            part = eight(t, jnp.max)
            top = part if top is None else jnp.maximum(top, part)
        base = jnp.max(top, axis=0, keepdims=True) - LIFT
        total = None
        for start, size in spans(cols, tall):
            here = slice(start, start + size)
            e = jnp.exp2(slot[here, :] - base)
            e_ref[place // repeat, here, :] = e
            part = eight(e, jnp.sum)
            total = part if total is None else total + part
        log_sum = base + jnp.log2(jnp.sum(total, axis=0, keepdims=True))
        for k in range(repeat):
            lanes = slice(k * LANES, (k + 1) * LANES)
            l_ref[place + k : place + k + 1, :] = log_sum[:, lanes]
            top_ref[place + k : place + k + 1, :] = base[:, lanes] + LIFT

    each_pair(xs, t_ref, fill, visit)
    if merge:
        l_ref[...] = merged([jnp.concatenate([log[...] for log in before], axis=0), l_ref[...]])


def merged(pieces):
    top = functools.reduce(jnp.maximum, pieces)
    return top + jnp.log2(sum(jnp.exp2(piece - top) for piece in pieces))


def column_kernel(*refs, count, share, tall, orders, masks, log_cols, segments):
    xs, refs = refs[:count], refs[count:]
    logs, refs = refs[: len(orders)], refs[len(orders) :]
    sq_ref, *data, f_ref, col_ref, l_ref, sum_ref, top_ref, t_ref = refs
    calls = sum(len(segment) for segment in segments)
    held, data = data[: 2 * calls], data[2 * calls :]
    ys, biases = data[::2], data[1::2]
    rows, width = xs[0].shape
    alpha = 2.0 * SCALE / width
    repeat = t_ref.shape[2] // LANES
    tiles = f_ref.shape[0]
    for k in range(len(orders)):
        pieces = [log[order[k] * tiles : (order[k] + 1) * tiles, :] for log, order in zip(logs, orders)]
        l_ref[k * tiles : (k + 1) * tiles, :] = merged(pieces)
    f_ref[...] = sq_ref[...] / width - (EPS * LN2) * l_ref[:tiles, :] + EPS * log_cols

    def fill(slot, x):
        offset = 0
        for y_ref in ys:
            cols = y_ref.shape[0]
            slot[offset : offset + cols, :] = dots(y_ref[...], x)
            offset += cols

    def each(visit):
        def visit_all(slot, place):
            log_here = jnp.concatenate([l_ref[place + k : place + k + 1, :] for k in range(repeat)], axis=1)
            offset = 0
            for b_ref in biases:
                for start, size in spans(b_ref.shape[0], tall):
                    here = slice(offset + start, offset + start + size)
                    bias = across(b_ref[start : start + size, :], repeat)
                    visit(here, alpha * slot[here, :] + bias - log_here)
                offset += b_ref.shape[0]

        each_pair(xs, t_ref, fill, visit_all)

    def raise_top(here, values):
        top_ref[here, :] = jnp.maximum(top_ref[here, :], fold(values, jnp.maximum))

    def add_from_top(here, values):
        sum_ref[here, :] += fold(jnp.exp2(values - across(top_ref[here, :], repeat)), jnp.add)

    offset = 0
    for segment in segments:
        pieces = []
        for first in segment:
            held_ref, e_ref, *held = held
            logs_here = l_ref[first * tiles : first * tiles + held_ref.shape[0], :]
            weights = jnp.exp2(held_ref[...] - logs_here + LIFT)
            for k in range(e_ref.shape[0]):
                scale = [weights[k * repeat + i : k * repeat + i + 1, :] for i in range(repeat)]
                pieces.append((e_ref, k, jnp.concatenate(scale, axis=1)))

        def add(index, carry, pieces=pieces, offset=offset):
            start = pl.multiple_of(index * tall, tall)
            here = pl.ds(start, tall)
            parts = [fold(e_ref[k, here, :] * scale, jnp.add) for e_ref, k, scale in pieces]
            sum_ref[pl.ds(offset + start, tall), :] = functools.reduce(jnp.add, parts)
            return carry

        lax.fori_loop(0, e_ref.shape[1] // tall, add, 0)
        offset += e_ref.shape[1]
    least = jnp.min(jnp.sum(sum_ref[...], axis=1, keepdims=True))
    top_ref[...] = jnp.full(top_ref.shape, -2.0 * LIFT, jnp.float32)

    @pl.when(jnp.logical_not(least >= FLOOR))
    def _():
        top_ref[...] = jnp.full(top_ref.shape, -jnp.inf, jnp.float32)
        each(raise_top)
        top = jnp.max(top_ref[...], axis=1, keepdims=True)
        top_ref[...] = jnp.broadcast_to(top, top_ref.shape)
        sum_ref[...] = jnp.zeros(sum_ref.shape, jnp.float32)
        each(add_from_top)

    gen, dat = lax.axis_index("gen"), lax.axis_index("dat")
    n_gen = lax.axis_size("gen")
    col_ref[...] = jnp.full(col_ref.shape, NOTHING, jnp.float32)
    for k, mask in enumerate(masks):
        here = slice(k * share, (k + 1) * share)
        total = jnp.sum(sum_ref[here, :].T, axis=0, keepdims=True)
        place = (dat ^ mask[1]) * n_gen + (gen ^ mask[0])
        col_ref[pl.ds(place, 1), :] = top_ref[here, :].T[0:1, :] + jnp.log2(total)


def per_device(gen_samples, data_samples, data_potential):
    rows, width = gen_samples.shape
    n_gen, n_dat = lax.axis_size("gen"), lax.axis_size("dat")
    share = data_samples.shape[0]
    half = share * n_gen
    cols = 2 * half
    tiles = rows // LANES
    span = round_up(share, TILE) + TILE
    own_g = data_potential.reshape(1, share)
    message, column, held_g, held_x = pl.pallas_call(
        pack_kernel,
        out_shape=(
            jax.ShapeDtypeStruct((span, width), jnp.bfloat16),
            jax.ShapeDtypeStruct((span * (n_gen // 2), width), jnp.bfloat16),
            jax.ShapeDtypeStruct((1, share), jnp.float32),
            jax.ShapeDtypeStruct((rows, width), gen_samples.dtype),
        ),
        in_specs=[pl.BlockSpec(memory_space=pltpu.HBM)] * 3,
        scratch_shapes=[
            pltpu.VMEM((share, width), jnp.bfloat16),
            pltpu.VMEM((1, share), jnp.float32),
            pltpu.SemaphoreType.DMA((3,)),
        ],
        compiler_params=pltpu.CompilerParams(vmem_limit_bytes=4 * MIB),
    )(*[pltpu.with_memory_space_constraint(array, pltpu.HBM) for array in (data_samples, own_g, gen_samples)])
    xs, order = gather_gen(gen_samples)
    column, far = gather_column(message, column)
    xs[0] = held_x
    xs[1:], norm_x = lax.optimization_barrier((xs[1:], held_x))
    sq = pl.pallas_call(
        norm_kernel,
        out_shape=jax.ShapeDtypeStruct((tiles, LANES), jnp.float32),
        compiler_params=pltpu.CompilerParams(vmem_limit_bytes=8 * MIB),
        cost_estimate=pl.CostEstimate(flops=8 * rows * width * width, bytes_accessed=4 * MIB, transcendentals=0),
    )(norm_x)
    xs[1:], sq = lax.optimization_barrier((xs[1:], sq))
    tall = 64

    def cost(count):
        return pl.CostEstimate(
            flops=2 * rows * len(xs) * count * width,
            bytes_accessed=2 * (rows * len(xs) + count) * width,
            transcendentals=rows * len(xs) * count,
        )

    def row_pass(rows_of, parts, before=(), unpacked=None):
        count = unpacked[0].shape[0] if unpacked else len(parts) * half // 2
        logs_shape = jax.ShapeDtypeStruct((len(rows_of) * tiles, LANES), jnp.float32)
        unpacked_shapes = (
            jax.ShapeDtypeStruct((count, width), jnp.bfloat16),
            jax.ShapeDtypeStruct((count, LANES), jnp.float32),
        )
        log, top, e, *rest = pl.pallas_call(
            functools.partial(
                row_kernel,
                count=len(rows_of),
                share=share,
                tall=tall,
                merge=len(before),
                unpacked=unpacked is not None,
            ),
            out_shape=(
                logs_shape,
                logs_shape,
                jax.ShapeDtypeStruct((2 * len(rows_of), count, rows // 2), jnp.float32),
            )
            + (() if unpacked else unpacked_shapes),
            scratch_shapes=[pltpu.VMEM((2, count, rows // 2), jnp.float32)],
            compiler_params=pltpu.CompilerParams(vmem_limit_bytes=12 * MIB),
            cost_estimate=cost(count),
        )(*rows_of, *before, *(unpacked or parts))
        return log, [top, e], rest

    near = swap(column, "gen", 1)
    twin = swap(column, "dat", 1)
    log_own, held_own, data = row_pass(xs[:1], [column])
    log_others, held_others, _ = row_pass(xs[1:], [], unpacked=data)
    near, log_own, log_others = lax.optimization_barrier((near, log_own, log_others))
    near_twin = swap(near, "dat", 1)
    twin, near = lax.optimization_barrier((twin, near))
    log, held_both, more = row_pass(xs, [near, twin], [log_own, log_others])
    data = data + more
    near_twin, log = lax.optimization_barrier((near_twin, log))
    log, held_last, more = row_pass(xs, [near_twin], [log])
    data = data + more
    held = held_own + held_others + held_both + held_last
    segments = [[0, 1], [0], [0]]
    masks = [(g ^ a, b) for a, b in ((0, 0), (1, 0), (0, 1), (1, 1)) for g in far]
    logs = [log]
    logs += [swap(logs[0], "dat", m) for m in order[1:]]
    orders = [[order.index(m ^ partner) for m in order] for partner in order]
    f, col = pl.pallas_call(
        functools.partial(
            column_kernel,
            count=len(xs),
            share=share,
            tall=tall,
            orders=orders,
            masks=masks,
            log_cols=math.log(half * n_dat),
            segments=segments,
        ),
        out_shape=(
            jax.ShapeDtypeStruct((tiles, LANES), jnp.float32),
            jax.ShapeDtypeStruct((n_dat * n_gen, share), jnp.float32),
        ),
        scratch_shapes=[
            pltpu.VMEM((len(order) * tiles, LANES), jnp.float32),
            pltpu.VMEM((cols, LANES), jnp.float32),
            pltpu.VMEM((cols, LANES), jnp.float32),
            pltpu.VMEM((2, cols, rows // 2), jnp.float32),
        ],
        compiler_params=pltpu.CompilerParams(vmem_limit_bytes=16 * MIB),
        cost_estimate=cost(cols),
    )(*xs, *logs, sq, *held, *data)
    totals = lax.all_to_all(col, ("dat", "gen"), 0, 0, tiled=True)
    top = jnp.max(totals, axis=0)
    total = top + jnp.log2(jnp.sum(jnp.exp2(totals - top[None, :]), axis=0))
    new_data = held_g[0] - (EPS * LN2) * total + EPS * math.log(rows * n_gen / half)
    return f.reshape(rows), new_data


def solution(mesh):
    in_specs = (P(("gen", "dat"), None), P(("dat", "gen"), None), P(("dat", "gen")))
    out_specs = (P(("gen", "dat")), P(("dat", "gen")))
    return jax.shard_map(per_device, mesh=mesh, in_specs=in_specs, out_specs=out_specs, check_vma=False)
```

```python
import functools
import math

import jax
import jax.numpy as jnp
from jax import lax
from jax.experimental import pallas as pl
from jax.experimental.pallas import tpu as pltpu
from jax.sharding import PartitionSpec as P

EPS = 0.05
LOG2E = 1.4426950408889634
LN2 = 0.6931471805599453
SCALE = LOG2E / EPS
LANES = 128
TILE = 16
LIFT = 50.0
FLOOR = 2.0**-41
MIB = 1024 * 1024
NOTHING = -1e30


def round_up(value, step):
    return -(-value // step) * step


def swap(value, axis, mask):
    return lax.ppermute(value, axis, [(k, k ^ mask) for k in range(lax.axis_size(axis))])


def gather_gen(gen_own):
    gens = [(gen_own, 0)]
    bit = lax.axis_size("dat") // 2
    while bit > 1:
        gens += [(swap(array, "dat", bit), mask ^ bit) for array, mask in gens]
        bit //= 2
    return [array for array, _ in gens], [mask for _, mask in gens]


def gather_column(message, column):
    span = message.shape[0]
    far = range(2, lax.axis_size("gen"), 2)
    for k, mask in enumerate(far):
        column = lax.dynamic_update_slice(column, swap(message, "gen", mask), ((k + 1) * span, 0))
    return column, [0, *far]


def pack_kernel(
    y_hbm_ref, g_hbm_ref, x_hbm_ref, packed_ref, column_ref, own_g_ref, own_x_ref, y_ref, g_ref, sems
):
    copies = [
        pltpu.make_async_copy(y_hbm_ref, y_ref, sems.at[0]),
        pltpu.make_async_copy(g_hbm_ref, g_ref, sems.at[1]),
        pltpu.make_async_copy(x_hbm_ref, own_x_ref, sems.at[2]),
    ]
    for copy in copies:
        copy.start()
    for copy in copies[:2]:
        copy.wait()
    share, width = y_ref.shape
    tall = packed_ref.shape[0] - TILE
    own_g_ref[...] = g_ref[...]
    y = y_ref[...]
    wide = y.astype(jnp.float32)
    sq = jnp.sum(wide * wide, axis=1, keepdims=True)
    sq = jnp.broadcast_to(sq, (share, LANES)).T[0:1, :]
    bias = SCALE * (g_ref[...] - sq / width)
    first = bias.astype(jnp.bfloat16).astype(jnp.float32)
    rest = bias - first
    second = rest.astype(jnp.bfloat16).astype(jnp.float32)
    third = rest - second
    row = lax.broadcasted_iota(jnp.int32, (TILE, share), 0)
    pieces = jnp.where(row == 0, first, jnp.where(row == 1, second, jnp.where(row == 2, third, 0.0)))
    if share < tall:
        packed_ref[...] = jnp.zeros(packed_ref.shape, jnp.bfloat16)
    else:
        packed_ref[tall:, :] = jnp.zeros((TILE, width), jnp.bfloat16)
    packed_ref[:share, :] = y
    packed_ref[tall:, :share] = pieces.astype(jnp.bfloat16)
    column_ref[: packed_ref.shape[0], :] = packed_ref[...]
    copies[2].wait()


def unpack(parts, share, y_ref, b_ref):
    tall = round_up(share, TILE)
    span = tall + TILE
    batch = TILE // math.gcd(share, TILE)
    held = []
    k = 0
    for part in parts:
        for start in range(0, part.shape[0], span):
            pieces = part[start + tall : start + span, :share].astype(jnp.float32)
            bias = pieces[0:1, :] + pieces[1:2, :] + pieces[2:3, :]
            b_ref[k * share : (k + 1) * share, :] = jnp.broadcast_to(bias, (LANES, share)).T
            if batch == 1:
                y_ref[k * share : (k + 1) * share, :] = part[start : start + share, :]
            else:
                held.append(part[start : start + tall, :].astype(jnp.float32)[:share, :])
                if len(held) == batch:
                    end = (k + 1) * share
                    y_ref[end - batch * share : end, :] = jnp.concatenate(held, axis=0).astype(jnp.bfloat16)
                    held = []
            k += 1


def norm_kernel(x_ref, sq_ref):
    x = x_ref[...].astype(jnp.float32)
    square = x * x
    high = square.astype(jnp.bfloat16)
    low = (square - high.astype(jnp.float32)).astype(jnp.bfloat16)
    ones = jnp.ones((TILE, x.shape[1]), jnp.bfloat16)
    sq = jnp.zeros((TILE, x.shape[0]), jnp.float32)
    for half in (high, low):
        sq += lax.dot_general(ones, half, (((1,), (1,)), ((), ())), preferred_element_type=jnp.float32)
    for k in range(sq_ref.shape[0]):
        sq_ref[k : k + 1, :] = sq[0:1, k * LANES : (k + 1) * LANES]


def spans(total, step):
    return [(start, min(step, total - start)) for start in range(0, total, step)]


def dots(y, x):
    return lax.dot_general(y, x, (((1,), (1,)), ((), ())), preferred_element_type=jnp.float32)


def across(values, count):
    return jnp.concatenate([values] * count, axis=1)


def each_pair(xs, dots_ref, fill, visit):
    rows = xs[0].shape[0]
    half = rows // 2
    for place, x_ref in enumerate(xs):
        for k in range(2):
            fill(dots_ref.at[k], x_ref[k * half : (k + 1) * half, :])
        for k in range(2):
            visit(dots_ref.at[k], (place * rows + k * half) // LANES)


def eight(values, op):
    groups = values.reshape(values.shape[0] // 8, 8, values.shape[1])
    return op(groups, axis=0)


def fold(values, op):
    out = values[:, :LANES]
    for start in range(LANES, values.shape[1], LANES):
        out = op(out, values[:, start : start + LANES])
    return out


def row_kernel(*refs, count, share, tall, merge, unpacked):
    xs, refs = refs[:count], refs[count:]
    before, refs = refs[:merge], refs[merge:]
    if unpacked:
        y_ref, b_ref, l_ref, top_ref, e_ref, t_ref = refs
    else:
        *parts, l_ref, top_ref, e_ref, y_ref, b_ref, t_ref = refs
        unpack(parts, share, y_ref, b_ref)
    cols, width = y_ref.shape
    alpha = 2.0 * SCALE / width
    repeat = t_ref.shape[2] // LANES

    def fill(slot, x):
        slot[...] = dots(y_ref[...], x)

    def visit(slot, place):
        top = None
        for start, size in spans(cols, tall):
            here = slice(start, start + size)
            t = alpha * slot[here, :] + across(b_ref[here, :], repeat)
            slot[here, :] = t
            part = eight(t, jnp.max)
            top = part if top is None else jnp.maximum(top, part)
        base = jnp.max(top, axis=0, keepdims=True) - LIFT
        total = None
        for start, size in spans(cols, tall):
            here = slice(start, start + size)
            e = jnp.exp2(slot[here, :] - base)
            e_ref[place // repeat, here, :] = e
            part = eight(e, jnp.sum)
            total = part if total is None else total + part
        log_sum = base + jnp.log2(jnp.sum(total, axis=0, keepdims=True))
        for k in range(repeat):
            lanes = slice(k * LANES, (k + 1) * LANES)
            l_ref[place + k : place + k + 1, :] = log_sum[:, lanes]
            top_ref[place + k : place + k + 1, :] = base[:, lanes] + LIFT

    each_pair(xs, t_ref, fill, visit)
    if merge:
        l_ref[...] = merged([jnp.concatenate([log[...] for log in before], axis=0), l_ref[...]])


def merged(pieces):
    top = functools.reduce(jnp.maximum, pieces)
    return top + jnp.log2(sum(jnp.exp2(piece - top) for piece in pieces))


def column_kernel(*refs, count, share, tall, orders, masks, log_cols, segments):
    xs, refs = refs[:count], refs[count:]
    logs, refs = refs[: len(orders)], refs[len(orders) :]
    sq_ref, *data, f_ref, col_ref, l_ref, sum_ref, top_ref, t_ref = refs
    calls = sum(len(segment) for segment in segments)
    held, data = data[: 2 * calls], data[2 * calls :]
    ys, biases = data[::2], data[1::2]
    rows, width = xs[0].shape
    alpha = 2.0 * SCALE / width
    repeat = t_ref.shape[2] // LANES
    tiles = f_ref.shape[0]
    for k in range(len(orders)):
        pieces = [log[order[k] * tiles : (order[k] + 1) * tiles, :] for log, order in zip(logs, orders)]
        l_ref[k * tiles : (k + 1) * tiles, :] = merged(pieces)
    f_ref[...] = sq_ref[...] / width - (EPS * LN2) * l_ref[:tiles, :] + EPS * log_cols

    def fill(slot, x):
        offset = 0
        for y_ref in ys:
            cols = y_ref.shape[0]
            slot[offset : offset + cols, :] = dots(y_ref[...], x)
            offset += cols

    def each(visit):
        def visit_all(slot, place):
            log_here = jnp.concatenate([l_ref[place + k : place + k + 1, :] for k in range(repeat)], axis=1)
            offset = 0
            for b_ref in biases:
                for start, size in spans(b_ref.shape[0], tall):
                    here = slice(offset + start, offset + start + size)
                    bias = across(b_ref[start : start + size, :], repeat)
                    visit(here, alpha * slot[here, :] + bias - log_here)
                offset += b_ref.shape[0]

        each_pair(xs, t_ref, fill, visit_all)

    def raise_top(here, values):
        top_ref[here, :] = jnp.maximum(top_ref[here, :], fold(values, jnp.maximum))

    def add_from_top(here, values):
        sum_ref[here, :] += fold(jnp.exp2(values - across(top_ref[here, :], repeat)), jnp.add)

    offset = 0
    for segment in segments:
        pieces = []
        for first in segment:
            held_ref, e_ref, *held = held
            logs_here = l_ref[first * tiles : first * tiles + held_ref.shape[0], :]
            weights = jnp.exp2(held_ref[...] - logs_here + LIFT)
            for k in range(e_ref.shape[0]):
                scale = [weights[k * repeat + i : k * repeat + i + 1, :] for i in range(repeat)]
                pieces.append((e_ref, k, jnp.concatenate(scale, axis=1)))

        stride = math.gcd(e_ref.shape[1], 3 * tall)

        def add(index, carry, pieces=pieces, offset=offset, stride=stride):
            start = pl.multiple_of(index * stride, stride)
            here = pl.ds(start, stride)
            parts = [fold(e_ref[k, here, :] * scale, jnp.add) for e_ref, k, scale in pieces]
            sum_ref[pl.ds(offset + start, stride), :] = functools.reduce(jnp.add, parts)
            return carry

        lax.fori_loop(0, e_ref.shape[1] // stride, add, 0)
        offset += e_ref.shape[1]
    least = jnp.min(jnp.sum(sum_ref[...], axis=1, keepdims=True))
    top_ref[...] = jnp.full(top_ref.shape, -2.0 * LIFT, jnp.float32)

    @pl.when(jnp.logical_not(least >= FLOOR))
    def _():
        top_ref[...] = jnp.full(top_ref.shape, -jnp.inf, jnp.float32)
        each(raise_top)
        top = jnp.max(top_ref[...], axis=1, keepdims=True)
        top_ref[...] = jnp.broadcast_to(top, top_ref.shape)
        sum_ref[...] = jnp.zeros(sum_ref.shape, jnp.float32)
        each(add_from_top)

    gen, dat = lax.axis_index("gen"), lax.axis_index("dat")
    n_gen = lax.axis_size("gen")
    col_ref[...] = jnp.full(col_ref.shape, NOTHING, jnp.float32)
    for k, mask in enumerate(masks):
        here = slice(k * share, (k + 1) * share)
        total = jnp.sum(sum_ref[here, :].T, axis=0, keepdims=True)
        place = (dat ^ mask[1]) * n_gen + (gen ^ mask[0])
        col_ref[pl.ds(place, 1), :] = top_ref[here, :].T[0:1, :] + jnp.log2(total)


def per_device(gen_samples, data_samples, data_potential):
    rows, width = gen_samples.shape
    n_gen, n_dat = lax.axis_size("gen"), lax.axis_size("dat")
    share = data_samples.shape[0]
    half = share * n_gen
    cols = 2 * half
    tiles = rows // LANES
    span = round_up(share, TILE) + TILE
    own_g = data_potential.reshape(1, share)
    message, column, held_g, held_x = pl.pallas_call(
        pack_kernel,
        out_shape=(
            jax.ShapeDtypeStruct((span, width), jnp.bfloat16),
            jax.ShapeDtypeStruct((span * (n_gen // 2), width), jnp.bfloat16),
            jax.ShapeDtypeStruct((1, share), jnp.float32),
            jax.ShapeDtypeStruct((rows, width), gen_samples.dtype),
        ),
        in_specs=[pl.BlockSpec(memory_space=pltpu.HBM)] * 3,
        scratch_shapes=[
            pltpu.VMEM((share, width), jnp.bfloat16),
            pltpu.VMEM((1, share), jnp.float32),
            pltpu.SemaphoreType.DMA((3,)),
        ],
        compiler_params=pltpu.CompilerParams(vmem_limit_bytes=4 * MIB),
    )(*[pltpu.with_memory_space_constraint(array, pltpu.HBM) for array in (data_samples, own_g, gen_samples)])
    xs, order = gather_gen(gen_samples)
    column, far = gather_column(message, column)
    xs[0] = held_x
    xs[1:], norm_x = lax.optimization_barrier((xs[1:], held_x))
    sq = pl.pallas_call(
        norm_kernel,
        out_shape=jax.ShapeDtypeStruct((tiles, LANES), jnp.float32),
        compiler_params=pltpu.CompilerParams(vmem_limit_bytes=8 * MIB),
        cost_estimate=pl.CostEstimate(flops=8 * rows * width * width, bytes_accessed=4 * MIB, transcendentals=0),
    )(norm_x)
    xs[1:], sq = lax.optimization_barrier((xs[1:], sq))
    tall = 64

    def cost(count):
        return pl.CostEstimate(
            flops=2 * rows * len(xs) * count * width,
            bytes_accessed=2 * (rows * len(xs) + count) * width,
            transcendentals=rows * len(xs) * count,
        )

    def row_pass(rows_of, parts, before=(), unpacked=None):
        count = unpacked[0].shape[0] if unpacked else len(parts) * half // 2
        logs_shape = jax.ShapeDtypeStruct((len(rows_of) * tiles, LANES), jnp.float32)
        unpacked_shapes = (
            jax.ShapeDtypeStruct((count, width), jnp.bfloat16),
            jax.ShapeDtypeStruct((count, LANES), jnp.float32),
        )
        log, top, e, *rest = pl.pallas_call(
            functools.partial(
                row_kernel,
                count=len(rows_of),
                share=share,
                tall=tall,
                merge=len(before),
                unpacked=unpacked is not None,
            ),
            out_shape=(
                logs_shape,
                logs_shape,
                jax.ShapeDtypeStruct((2 * len(rows_of), count, rows // 2), jnp.float32),
            )
            + (() if unpacked else unpacked_shapes),
            scratch_shapes=[pltpu.VMEM((2, count, rows // 2), jnp.float32)],
            compiler_params=pltpu.CompilerParams(vmem_limit_bytes=12 * MIB),
            cost_estimate=cost(count),
        )(*rows_of, *before, *(unpacked or parts))
        return log, [top, e], rest

    near = swap(column, "gen", 1)
    twin = swap(column, "dat", 1)
    log_own, held_own, data = row_pass(xs[:1], [column])
    log_others, held_others, _ = row_pass(xs[1:], [], unpacked=data)
    near, log_own, log_others = lax.optimization_barrier((near, log_own, log_others))
    near_twin = swap(near, "dat", 1)
    twin, near = lax.optimization_barrier((twin, near))
    log, held_both, more = row_pass(xs, [near, twin], [log_own, log_others])
    data = data + more
    near_twin, log = lax.optimization_barrier((near_twin, log))
    log, held_last, more = row_pass(xs, [near_twin], [log])
    data = data + more
    held = held_own + held_others + held_both + held_last
    segments = [[0, 1], [0], [0]]
    masks = [(g ^ a, b) for a, b in ((0, 0), (1, 0), (0, 1), (1, 1)) for g in far]
    logs = [log]
    logs += [swap(logs[0], "dat", m) for m in order[1:]]
    orders = [[order.index(m ^ partner) for m in order] for partner in order]
    f, col = pl.pallas_call(
        functools.partial(
            column_kernel,
            count=len(xs),
            share=share,
            tall=tall,
            orders=orders,
            masks=masks,
            log_cols=math.log(half * n_dat),
            segments=segments,
        ),
        out_shape=(
            jax.ShapeDtypeStruct((tiles, LANES), jnp.float32),
            jax.ShapeDtypeStruct((n_dat * n_gen, share), jnp.float32),
        ),
        scratch_shapes=[
            pltpu.VMEM((len(order) * tiles, LANES), jnp.float32),
            pltpu.VMEM((cols, LANES), jnp.float32),
            pltpu.VMEM((cols, LANES), jnp.float32),
            pltpu.VMEM((2, cols, rows // 2), jnp.float32),
        ],
        compiler_params=pltpu.CompilerParams(vmem_limit_bytes=16 * MIB),
        cost_estimate=cost(cols),
    )(*xs, *logs, sq, *held, *data)
    totals = lax.all_to_all(col, ("dat", "gen"), 0, 0, tiled=True)
    top = jnp.max(totals, axis=0)
    total = top + jnp.log2(jnp.sum(jnp.exp2(totals - top[None, :]), axis=0))
    new_data = held_g[0] - (EPS * LN2) * total + EPS * math.log(rows * n_gen / half)
    return f.reshape(rows), new_data


def solution(mesh):
    in_specs = (P(("gen", "dat"), None), P(("dat", "gen"), None), P(("dat", "gen")))
    out_specs = (P(("gen", "dat")), P(("dat", "gen")))
    return jax.shard_map(per_device, mesh=mesh, in_specs=in_specs, out_specs=out_specs, check_vma=False)
```
